256 devices in a mesh: fsdp: 32 (over z, y), tensor: 8 (over x, core).
Axes of the slice: x: 4, y: 4, z: 8, core: 2. Of those that a mesh axis runs over, the one named last changes fastest.
Arguments:
- momentum: float32 [16384, 9216], P('fsdp', 'tensor'), may hold values from -6 to 6
- gradient: bfloat16 [16384, 9216], P('fsdp', 'tensor'), may hold values from -3 to 3
- weights: float32 [16384, 9216], P('fsdp', 'tensor'), may hold values from -6 to 6
- prior_right: float32 [9216, 256], P('tensor'), may hold values from -6 to 6
Outputs:
- new_momentum: float32 [16384, 9216], P('fsdp', 'tensor')
- new_weights: float32 [16384, 9216], P('fsdp', 'tensor')
- new_right: float32 [9216, 256], P('tensor')
The draws below stay inside these ranges and needn't reach their ends.
All inputs are finite; a program needn't handle non-finite values.
Results may differ from the reference program's by a relative error of at most 0.0003.
Values sent between devices are 32-bit elements; how exact they have to be, the bound alone decides.
A program may use at most 64 MiB of HBM per device.

```python
import math
import jax
import jax.numpy as jnp
from jax import lax

ROWS = 16384
COLS = 9216
RANK = 256


def level_of(rng, dims, pieces, least, high):
    factor_of, own = 1.0, jax.random.fold_in(rng, 6)
    for axis_at, blocks in pieces:
        steps = jnp.exp(jax.random.uniform(jax.random.fold_in(own, axis_at), (blocks,), jnp.float32, least / len(pieces), high / len(pieces)))
        factor_of = factor_of * jnp.repeat(steps, dims[axis_at] // blocks).reshape([-1 if axis == axis_at else 1 for axis in range(len(dims))])
    return factor_of


def noise(key, dims, scale, reach, split=(), dtype=jnp.bfloat16):
    values = scale * jax.random.normal(key, dims, jnp.float32)
    if split:
        values = values * level_of(key, dims, split, -0.22, 0.18)
    return jnp.clip(values, -reach, reach).astype(dtype)


def setup_inputs(seed: int = 0) -> dict:
    streams_of = jax.random.split(jax.random.key(seed), 5)
    momentum = noise(streams_of[0], (ROWS, COLS), 1.0, 6.0, ((0, 32), (1, 8)), jnp.float32)
    gradient = noise(streams_of[1], (ROWS, COLS), 0.5, 3.0, ((0, 32), (1, 8)))
    weights = noise(streams_of[2], (ROWS, COLS), 1.0, 6.0, ((0, 32), (1, 8)), jnp.float32)
    prior_right = noise(streams_of[3], (COLS, RANK), 1.0, 6.0, ((0, 8),), jnp.float32)
    return {"momentum": momentum, "gradient": gradient, "weights": weights, "prior_right": prior_right}


def matmul_high(left_mat, right_mat):
    return jnp.dot(left_mat.astype(jnp.float32), right_mat.astype(jnp.float32), precision=lax.Precision.HIGHEST, preferred_element_type=jnp.float32)

def reference(momentum, gradient, weights, prior_right):
    buffer = momentum + gradient.astype(jnp.float32)
    projected = matmul_high(buffer, prior_right)
    basis_raw, upper = jnp.linalg.qr(projected)
    signs = jnp.sign(jnp.diagonal(upper))
    ortho_basis = basis_raw * signs[None, :]
    right_factor = matmul_high(buffer.T, ortho_basis)
    col_scale = lax.rsqrt(lax.optimization_barrier(jnp.mean(right_factor * right_factor, axis=0)) + 1e-06)
    new_right = right_factor * col_scale[None, :]
    new_momentum = buffer - 0.5 * matmul_high(ortho_basis, right_factor.T)
    step_size = 0.2 * math.sqrt(ROWS / RANK)
    new_weights = weights - step_size * matmul_high(ortho_basis, new_right.T)
    return (new_momentum, new_weights, new_right)
```

```python
import functools
import math

import jax
import jax.numpy as jnp
from jax import lax
from jax.experimental import pallas as pl
from jax.experimental.pallas import tpu as pltpu
from jax.sharding import PartitionSpec as P

ROWS = 16384
COLS = 9216
RANK = 256
NZ, NY, NX = 8, 4, 4
BR = 512
BC = 1152
HALF = 128
LEAF = 64
PANEL = 16
F32 = jnp.float32
BF16 = jnp.bfloat16
MESH = pl.DeviceIdType.MESH
CHUNKS = ((0, 256, "z"), (256, 512, "y"), (768, 384, "y"))


def dot_f32(a, b, ca, cb):
    return lax.dot_general(
        a, b, (((ca,), (cb,)), ((), ())), precision=lax.Precision.HIGHEST, preferred_element_type=F32
    )


def split(a):
    hi = a.astype(BF16)
    return hi, (a - hi.astype(F32)).astype(BF16)


def dot_bf16(a, b, ca, cb):
    return lax.dot_general(a, b, (((ca,), (cb,)), ((), ())), preferred_element_type=F32)


def dot3(a, b, ca, cb):
    return dot_bf16(a[0], b[0], ca, cb) + (dot_bf16(a[0], b[1], ca, cb) + dot_bf16(a[1], b[0], ca, cb))


def leaf_elimination(block):
    n = block.shape[0]
    row = lax.broadcasted_iota(jnp.int32, (n, n), 0)
    lane = lax.broadcasted_iota(jnp.int32, (n, n), 1)
    for p0 in range(0, n, PANEL):
        cols = [jnp.broadcast_to(block[p0:, p0 + j : p0 + j + 1], (n - p0, n)) for j in range(PANEL)]
        rw, ln, low = row[p0:], lane[p0:], block[p0:]
        for k in range(PANEL):
            r = 1.0 / cols[k][k : k + 1, :]
            f = jnp.where(rw > p0 + k, cols[k] * r, 0.0)
            for j in range(k + 1, PANEL):
                cols[j] = cols[j] - f * cols[j][k : k + 1, :]
            pivot_row = jnp.where(ln[0:1] == p0 + k, 1.0, low[k : k + 1, :])
            cleared = jnp.where((ln == p0 + k) & (rw > p0 + k), 0.0, low)
            low = cleared - f * pivot_row
        block = jnp.concatenate([block[:p0], low], axis=0) if p0 else low
    return block


def cholesky_inverse(a, between):
    blocks = RANK // LEAF
    for j in range(blocks):
        s = slice(j * LEAF, (j + 1) * LEAF)
        d = leaf_elimination(a[s, s])
        row = lax.broadcasted_iota(jnp.int32, (LEAF, LEAF), 0)
        lane = lax.broadcasted_iota(jnp.int32, (LEAF, LEAF), 1)
        pivot = jnp.sum(jnp.where(row == lane, d, 0.0), axis=1, keepdims=True)
        unit = jnp.where(row > lane, d, jnp.where(row == lane, 1.0, 0.0))
        inv = unit * lax.rsqrt(pivot)
        x = dot_f32(inv, a[s, :], 1, 0)
        a[s, :] = x
        a[s, s] = inv
        if j < blocks - 1:
            low = (j + 1) * LEAF
            a[low:, s] = jnp.zeros((RANK - low, LEAF), F32)
            a[low:, :] = a[low:, :] - dot_f32(x[:, low:], a[s, :], 0, 0)
            between(j)


def factor_kernel(
    m_ref, g_ref, v_ref, q_ref, rt_ref, norm_ref,
    bh, bl, part, crecv, half, xrecv, own, pfull, pt,
    gpart, gyrecv, gz, gmat,
    w, wf, r1y, r1z, s1y, s1z, r2y, r2z, s2,
    nbuf, c_s, c_r, x_s, x_r, g_s, g_r, w_s, w_r, n_s, n_r,
):
    fi, ti = lax.axis_index("fsdp"), lax.axis_index("tensor")
    z, y = fi // NY, lax.rem(fi, NY)
    x, c = ti // 2, lax.rem(ti, 2)

    def dev(zz, yy, xx, cc):
        return (zz * NY + yy, xx * 2 + cc)

    def peer_z(i):
        return lax.rem(z + i, NZ)

    def peer_y(i):
        return lax.rem(y + i, NY)

    def peer_x(i):
        return lax.rem(x + i, NX)

    pending = []

    def send(src, dst, ss, rs, to):
        copy = pltpu.make_async_remote_copy(
            src_ref=src, dst_ref=dst, send_sem=ss, recv_sem=rs, device_id=to, device_id_type=MESH
        )
        copy.start()
        pending.append(copy)
        return copy

    barrier = pltpu.get_barrier_semaphore()
    peers = [dev(z, peer_y(i), x, c) for i in range(1, NY)]
    peers += [dev(peer_z(i), y, x, c) for i in range(1, NZ)]
    tensor_peers = [dev(z, y, x, 1 - c)]
    tensor_peers += [dev(z, y, peer_x(i), cc) for i in range(1, NX) for cc in (c, 1 - c)]
    for p in peers + tensor_peers:
        pl.semaphore_signal(barrier, inc=1, device_id=p, device_id_type=MESH)

    buf = m_ref[...] + g_ref[...].astype(F32)
    bh[...], bl[...] = split(buf)

    def ds(start, size):
        return pl.ds(pl.multiple_of(start, 8), size)

    core_rs, x_rs, x_ag, core_ag = [], [], [], []
    for h in range(2):
        vh = split(v_ref[:, h * HALF : (h + 1) * HALF])
        part[h] = dot3((bh[...], bl[...]), vh, 1, 0)
        if h == 0:
            pl.semaphore_wait(barrier, len(peers + tensor_peers))
        core_rs.append(
            send(part.at[h, ds(256 * (1 - c), 256)], crecv.at[h], c_s.at[h, 0], c_r.at[h, 0], dev(z, y, x, 1 - c))
        )
    for h in range(2):
        core_rs[h].wait_recv()
        half[h] = part[h, ds(256 * c, 256), :] + crecv[h]
        x_rs.append([
            send(half.at[h, ds(64 * peer_x(i), 64)], xrecv.at[h, i - 1], x_s.at[h, 0, i - 1], x_r.at[h, 0, i - 1],
                 dev(z, y, peer_x(i), c))
            for i in range(1, NX)
        ])
    for h in range(2):
        for cp in x_rs[h]:
            cp.wait_recv()
        total = half[h, ds(64 * x, 64), :]
        for i in range(NX - 1):
            total = total + xrecv[h, i]
        own[h] = total
        at = 256 * c + 64 * x
        x_ag.append([
            send(own.at[h], pfull.at[h, ds(at, 64)], x_s.at[h, 1, i - 1], x_r.at[h, 1, i - 1], dev(z, y, peer_x(i), c))
            for i in range(1, NX)
        ])
        core_ag.append([
            send(own.at[h], pfull.at[h, ds(at, 64)], c_s.at[h, 1], c_r.at[h, 1], dev(z, y, x, 1 - c))
        ])
        pfull[h, ds(at, 64), :] = total
    for h in range(2):
        for i in range(1, NX):
            x_ag[h][i - 1].wait_recv()
            at = 256 * c + 64 * lax.rem(x + NX - i, NX)
            core_ag[h].append(
                send(pfull.at[h, ds(at, 64)], pfull.at[h, ds(at, 64)], c_s.at[h, 1 + i], c_r.at[h, 1 + i],
                     dev(z, y, x, 1 - c))
            )
        for cp in core_ag[h]:
            cp.wait_recv()
        ph = pfull[h].T
        pt[h * HALF : (h + 1) * HALF, :] = ph
        w[h * HALF : (h + 1) * HALF, :] = dot3(split(ph), (bh[...], bl[...]), 1, 0)

    rows = ds(32 * ti, 32)
    ptr = pt[rows, :]
    for h in range(2):
        gpart[:, h * HALF : (h + 1) * HALF] = dot_f32(ptr, pfull[h], 1, 0)
    g1 = [
        send(gpart.at[ds(8 * peer_y(i), 8)], gyrecv.at[i - 1], g_s.at[0, i - 1], g_r.at[0, i - 1],
             dev(z, peer_y(i), x, c))
        for i in range(1, NY)
    ]

    def to_y(i):
        return dev(z, peer_y(i), x, c)

    def to_z(i):
        return dev(peer_z(i), y, x, c)

    rs1, rs2, ag1, ag2 = {}, {}, {}, {}

    def start_rs1(n):
        c0, nc, first = CHUNKS[n]
        cs = pl.ds(c0, nc)
        if first == "y":
            rs1[n] = [
                send(w.at[ds(64 * peer_y(i), 64), cs], r1y.at[i - 1, :, cs], w_s.at[n, 0, i - 1], w_r.at[n, 0, i - 1], to_y(i))
                for i in range(1, NY)
            ]
        else:
            rs1[n] = [
                send(w.at[ds(32 * peer_z(i), 32), cs], r1z.at[i - 1, :, cs], w_s.at[n, 0, i - 1], w_r.at[n, 0, i - 1], to_z(i))
                for i in range(1, NZ)
            ]

    def start_rs2(n):
        c0, nc, first = CHUNKS[n]
        cs = pl.ds(c0, nc)
        for cp in rs1[n]:
            cp.wait_recv()
        if first == "y":
            total = w[ds(64 * y, 64), cs]
            for i in range(NY - 1):
                total = total + r1y[i, :, cs]
            s1y[:, cs] = total
            rs2[n] = [
                send(s1y.at[ds(8 * peer_z(i), 8), cs], r2z.at[i - 1, :, cs], w_s.at[n, 1, i - 1], w_r.at[n, 1, i - 1], to_z(i))
                for i in range(1, NZ)
            ]
        else:
            total = w[ds(32 * z, 32), cs]
            for i in range(NZ - 1):
                total = total + r1z[i, :, cs]
            s1z[:, cs] = total
            rs2[n] = [
                send(s1z.at[ds(8 * peer_y(i), 8), cs], r2y.at[i - 1, :, cs], w_s.at[n, 1, i - 1], w_r.at[n, 1, i - 1], to_y(i))
                for i in range(1, NY)
            ]

    def start_ag1(n):
        c0, nc, first = CHUNKS[n]
        cs = pl.ds(c0, nc)
        for cp in rs2[n]:
            cp.wait_recv()
        if first == "y":
            total = s1y[ds(8 * z, 8), cs]
            for i in range(NZ - 1):
                total = total + r2z[i, :, cs]
            at = 64 * y + 8 * z
            s2[:, cs] = total
            ag1[n] = [
                send(s2.at[:, cs], wf.at[ds(at, 8), cs], w_s.at[n, 2, i - 1], w_r.at[n, 2, i - 1], to_z(i))
                for i in range(1, NZ)
            ]
        else:
            total = s1z[ds(8 * y, 8), cs]
            for i in range(NY - 1):
                total = total + r2y[i, :, cs]
            at = 32 * z + 8 * y
            s2[:, cs] = total
            ag1[n] = [
                send(s2.at[:, cs], wf.at[ds(at, 8), cs], w_s.at[n, 2, i - 1], w_r.at[n, 2, i - 1], to_y(i))
                for i in range(1, NY)
            ]
        wf[ds(at, 8), cs] = total

    def start_ag2(n):
        c0, nc, first = CHUNKS[n]
        cs = pl.ds(c0, nc)
        for cp in ag1[n]:
            cp.wait_recv()
        if first == "y":
            piece = wf.at[ds(64 * y, 64), cs]
            ag2[n] = [
                send(piece, piece, w_s.at[n, 3, i - 1], w_r.at[n, 3, i - 1], to_y(i)) for i in range(1, NY)
            ]
        else:
            piece = wf.at[ds(32 * z, 32), cs]
            ag2[n] = [
                send(piece, piece, w_s.at[n, 3, i - 1], w_r.at[n, 3, i - 1], to_z(i)) for i in range(1, NZ)
            ]

    order = range(len(CHUNKS))
    for n in order:
        start_rs1(n)

    for cp in g1:
        cp.wait_recv()
    total = gpart[ds(8 * y, 8), :]
    for i in range(NY - 1):
        total = total + gyrecv[i]
    gz[z] = total
    g2 = [send(gz.at[z], gz.at[z], g_s.at[1, i - 1], g_r.at[1, i - 1], to_z(i)) for i in range(1, NZ)]
    for cp in g2:
        cp.wait_recv()
    total = gz[0]
    for i in range(1, NZ):
        total = total + gz[i]
    mine = ds(32 * ti + 8 * y, 8)
    gmat[mine, :] = total
    g3 = [send(gmat.at[mine], gmat.at[mine], g_s.at[2, i - 1], g_r.at[2, i - 1], to_y(i)) for i in range(1, NY)]

    start_rs2(0)
    for cp in g3:
        cp.wait_recv()
    g4 = [send(gmat.at[rows], gmat.at[rows], g_s.at[3, i - 1], g_r.at[3, i - 1], dev(z, y, peer_x(i), c)) for i in range(1, NX)]
    g5 = [send(gmat.at[rows], gmat.at[rows], g_s.at[4, 0], g_r.at[4, 0], dev(z, y, x, 1 - c))]
    start_rs2(1)
    for i in range(1, NX):
        g4[i - 1].wait_recv()
        theirs = ds(64 * lax.rem(x + NX - i, NX) + 32 * c, 32)
        g5.append(send(gmat.at[theirs], gmat.at[theirs], g_s.at[4, i], g_r.at[4, i], dev(z, y, x, 1 - c)))
    start_rs2(2)
    for cp in g5:
        cp.wait_recv()
    for cp in g3 + g4 + g5:
        cp.wait_send()
    done = [id(cp) for cp in g3 + g4 + g5]
    pending[:] = [cp for cp in pending if id(cp) not in done]

    def between(j):
        if j == 0:
            for n in order:
                start_ag1(n)
        if j == 2:
            for n in order:
                start_ag2(n)

    cholesky_inverse(gmat, between)
    row = lax.broadcasted_iota(jnp.int32, (RANK, RANK), 0)
    lane = lax.broadcasted_iota(jnp.int32, (RANK, RANK), 1)
    inv = split(jnp.where(row >= lane, gmat[...], 0.0))
    for n in order:
        for cp in ag2[n]:
            cp.wait_recv()
    rt = dot3(inv, split(wf[...]), 1, 0)
    rt_ref[...] = rt
    squares = jnp.sum(rt * rt, axis=1, keepdims=True)
    nbuf[ti] = jnp.broadcast_to(squares, (RANK, 128))
    n1 = [send(nbuf.at[ti], nbuf.at[ti], n_s.at[i], n_r.at[i], p) for i, p in enumerate(tensor_peers)]
    q = dot3(split(pfull[0]), (inv[0][:, :HALF], inv[1][:, :HALF]), 1, 1)
    q_ref[...] = q + dot3(split(pfull[1]), (inv[0][:, HALF:], inv[1][:, HALF:]), 1, 1)
    for cp in n1:
        cp.wait_recv()
    total = nbuf[0]
    for i in range(1, 2 * NX):
        total = total + nbuf[i]
    norm_ref[...] = lax.rsqrt(total / COLS + 1e-06)
    for cp in pending:
        cp.wait_send()


def output_kernel(m_ref, g_ref, wt_ref, q_ref, rt_ref, norm_ref, nm_ref, nw_ref, nr_ref, rh, rl, nh, nl):
    @pl.when(pl.program_id(0) == 0)
    def _():
        rt = rt_ref[...]
        scaled = rt * norm_ref[:, 0:1]
        nr_ref[...] = scaled.T
        rh[...], rl[...] = split(rt)
        nh[...], nl[...] = split(scaled)

    q = split(q_ref[...])
    buf = m_ref[...] + g_ref[...].astype(F32)
    nm_ref[...] = buf - 0.5 * dot3(q, (rh[...], rl[...]), 1, 0)
    step_size = 0.2 * math.sqrt(ROWS / RANK)
    nw_ref[...] = wt_ref[...] - step_size * dot3(q, (nh[...], nl[...]), 1, 0)


def body(momentum, gradient, weights, prior_right):
    vmem = pl.BlockSpec(memory_space=pltpu.VMEM)
    nch = len(CHUNKS)
    dma = pltpu.SemaphoreType.DMA
    q, rt, norm = pl.pallas_call(
        factor_kernel,
        out_shape=(
            jax.ShapeDtypeStruct((BR, RANK), F32),
            jax.ShapeDtypeStruct((RANK, BC), F32),
            jax.ShapeDtypeStruct((RANK, 128), F32),
        ),
        in_specs=[vmem] * 3,
        out_specs=(vmem,) * 3,
        scratch_shapes=[
            pltpu.VMEM((BR, BC), BF16),
            pltpu.VMEM((BR, BC), BF16),
            pltpu.VMEM((2, BR, HALF), F32),
            pltpu.VMEM((2, 256, HALF), F32),
            pltpu.VMEM((2, 256, HALF), F32),
            pltpu.VMEM((2, NX - 1, 64, HALF), F32),
            pltpu.VMEM((2, 64, HALF), F32),
            pltpu.VMEM((2, BR, HALF), F32),
            pltpu.VMEM((RANK, BR), F32),
            pltpu.VMEM((32, RANK), F32),
            pltpu.VMEM((NY - 1, 8, RANK), F32),
            pltpu.VMEM((NZ, 8, RANK), F32),
            pltpu.VMEM((RANK, RANK), F32),
            pltpu.VMEM((RANK, BC), F32),
            pltpu.VMEM((RANK, BC), F32),
            pltpu.VMEM((NY - 1, 64, BC), F32),
            pltpu.VMEM((NZ - 1, 32, BC), F32),
            pltpu.VMEM((64, BC), F32),
            pltpu.VMEM((32, BC), F32),
            pltpu.VMEM((NY - 1, 8, BC), F32),
            pltpu.VMEM((NZ - 1, 8, BC), F32),
            pltpu.VMEM((8, BC), F32),
            pltpu.VMEM((2 * NX, RANK, 128), F32),
            dma((2, 5)), dma((2, 5)),
            dma((2, 2, 3)), dma((2, 2, 3)),
            dma((5, 7)), dma((5, 7)),
            dma((nch, 4, 7)), dma((nch, 4, 7)),
            dma((7,)), dma((7,)),
        ],
        compiler_params=pltpu.CompilerParams(
            collective_id=0, has_side_effects=True, vmem_limit_bytes=50 * 1024 * 1024
        ),
        name="factors",
    )(momentum, gradient, prior_right)
    tile = 128
    by_rows = pl.BlockSpec((tile, BC), lambda i: (i, 0))
    whole = lambda shape: pl.BlockSpec(shape, lambda i: (0, 0))
    return pl.pallas_call(
        output_kernel,
        grid=(BR // tile,),
        out_shape=(
            jax.ShapeDtypeStruct((BR, BC), F32),
            jax.ShapeDtypeStruct((BR, BC), F32),
            jax.ShapeDtypeStruct((BC, RANK), F32),
        ),
        in_specs=[
            by_rows, by_rows, by_rows,
            pl.BlockSpec((tile, RANK), lambda i: (i, 0)),
            whole((RANK, BC)), whole((RANK, 128)),
        ],
        out_specs=(by_rows, by_rows, whole((BC, RANK))),
        scratch_shapes=[pltpu.VMEM((RANK, BC), BF16)] * 4,
        compiler_params=pltpu.CompilerParams(vmem_limit_bytes=50 * 1024 * 1024),
        name="outputs",
    )(momentum, gradient, weights, q, rt, norm)


def solution(mesh):
    in_specs = (P("fsdp", "tensor"), P("fsdp", "tensor"), P("fsdp", "tensor"), P("tensor", None))
    out_specs = (P("fsdp", "tensor"), P("fsdp", "tensor"), P("tensor", None))
    return jax.shard_map(body, mesh=mesh, in_specs=in_specs, out_specs=out_specs, check_vma=False)
```

```python
import functools
import math

import jax
import jax.numpy as jnp
from jax import lax
from jax.experimental import pallas as pl
from jax.experimental.pallas import tpu as pltpu
from jax.sharding import PartitionSpec as P

ROWS = 16384
COLS = 9216
RANK = 256
NZ, NY, NX = 8, 4, 4
BR = 512
BC = 1152
HALF = 128
LEAF = 64
PANEL = 16
F32 = jnp.float32
BF16 = jnp.bfloat16
MESH = pl.DeviceIdType.MESH
CHUNKS = ((0, 256, "z"), (256, 384, "y"), (640, 256, "y"), (896, 256, "y"))


def dot_f32(a, b, ca, cb):
    return lax.dot_general(
        a, b, (((ca,), (cb,)), ((), ())), precision=lax.Precision.HIGHEST, preferred_element_type=F32
    )


def split(a):
    hi = a.astype(BF16)
    return hi, (a - hi.astype(F32)).astype(BF16)


def dot_bf16(a, b, ca, cb):
    return lax.dot_general(a, b, (((ca,), (cb,)), ((), ())), preferred_element_type=F32)


def dot3(a, b, ca, cb):
    return dot_bf16(
        jnp.concatenate([a[0], a[0], a[1]], axis=ca), jnp.concatenate([b[1], b[0], b[0]], axis=cb), ca, cb
    )


def leaf_elimination(block, service):
    n = block.shape[0]
    row = lax.broadcasted_iota(jnp.int32, (n, n), 0)
    lane = lax.broadcasted_iota(jnp.int32, (n, n), 1)
    for p0 in range(0, n, PANEL):
        cols = [jnp.broadcast_to(block[p0:, p0 + j : p0 + j + 1], (n - p0, n)) for j in range(PANEL)]
        rw, ln, low = row[p0:], lane[p0:], block[p0:]
        for k in range(PANEL):
            r = 1.0 / cols[k][k : k + 1, :]
            f = jnp.where(rw > p0 + k, cols[k] * r, 0.0)
            for j in range(k + 1, PANEL):
                cols[j] = cols[j] - f * cols[j][k : k + 1, :]
            pivot_row = jnp.where(ln[0:1] == p0 + k, 1.0, low[k : k + 1, :])
            cleared = jnp.where((ln == p0 + k) & (rw > p0 + k), 0.0, low)
            low = cleared - f * pivot_row
        block = jnp.concatenate([block[:p0], low], axis=0) if p0 else low
        service()
    return block


def cholesky_inverse(a, service):
    blocks = RANK // LEAF
    for j in range(blocks):
        s = slice(j * LEAF, (j + 1) * LEAF)
        d = leaf_elimination(a[s, s], service)
        row = lax.broadcasted_iota(jnp.int32, (LEAF, LEAF), 0)
        lane = lax.broadcasted_iota(jnp.int32, (LEAF, LEAF), 1)
        pivot = jnp.sum(jnp.where(row == lane, d, 0.0), axis=1, keepdims=True)
        unit = jnp.where(row > lane, d, jnp.where(row == lane, 1.0, 0.0))
        inv = unit * lax.rsqrt(pivot)
        x = dot_f32(inv, a[s, :], 1, 0)
        a[s, :] = x
        a[s, s] = inv
        if j < blocks - 1:
            low = (j + 1) * LEAF
            a[low:, s] = jnp.zeros((RANK - low, LEAF), F32)
            a[low:, :] = a[low:, :] - dot_f32(x[:, low:], a[s, :], 0, 0)


def factor_kernel(
    m_ref, g_ref, wt_ref, v_ref, nm_ref, wv_ref, q_ref, rh_ref, rl_ref, rtt_ref, norm_ref,
    mv, gv, vv, bh, bl, part, crecv, half, xrecv, own, pfull, pt,
    gpart, gyrecv, gz, gmat,
    w, wf, r1y, r1z, s1y, s1z, r2y, r2z, s2,
    nbuf, l_s, c_s, c_r, x_s, x_r, g_s, g_r, w_s, w_r, n_s, n_r,
):
    fi, ti = lax.axis_index("fsdp"), lax.axis_index("tensor")
    z, y = fi // NY, lax.rem(fi, NY)
    x, c = ti // 2, lax.rem(ti, 2)

    def dev(zz, yy, xx, cc):
        return (zz * NY + yy, xx * 2 + cc)

    def peer_z(i):
        return lax.rem(z + i, NZ)

    def peer_y(i):
        return lax.rem(y + i, NY)

    def peer_x(i):
        return lax.rem(x + i, NX)

    def ds(start, size):
        return pl.ds(pl.multiple_of(start, size if size < 16 else 16), size)

    pending = []

    def send(src, dst, ss, rs, to):
        copy = pltpu.make_async_remote_copy(
            src_ref=src, dst_ref=dst, send_sem=ss, recv_sem=rs, device_id=to, device_id_type=MESH
        )
        copy.start()
        pending.append(copy)
        return copy

    load_v = pltpu.make_async_copy(v_ref, vv, l_s.at[0])
    load_v.start()
    loads = []
    for k, cc in enumerate((1 - c, c)):
        rows = ds(256 * cc, 256)
        loads.append([
            pltpu.make_async_copy(m_ref.at[rows], mv.at[k], l_s.at[1 + 2 * k]),
            pltpu.make_async_copy(g_ref.at[rows], gv.at[k], l_s.at[2 + 2 * k]),
        ])
        for cp in loads[k]:
            cp.start()

    load_w = pltpu.make_async_copy(wt_ref, wv_ref, l_s.at[5])
    load_w.start()

    barrier = pltpu.get_barrier_semaphore()
    peers = [dev(z, peer_y(i), x, c) for i in range(1, NY)]
    peers += [dev(peer_z(i), y, x, c) for i in range(1, NZ)]
    tensor_peers = [dev(z, y, x, 1 - c)]
    tensor_peers += [dev(z, y, peer_x(i), cc) for i in range(1, NX) for cc in (c, 1 - c)]
    plane_peers = [dev(z, peer_y(j), peer_x(i), c) for i in range(1, NX) for j in range(1, NY)]
    everyone = peers + tensor_peers + plane_peers
    for p in everyone:
        pl.semaphore_signal(barrier, inc=1, device_id=p, device_id_type=MESH)

    load_v.wait()
    vs = split(vv[...])

    def projected(k, cc):
        for cp in loads[k]:
            cp.wait()
        rows = ds(256 * cc, 256)
        hi, lo = split(mv[k] + gv[k].astype(F32))
        bh[rows, :] = hi
        bl[rows, :] = lo
        return dot3((hi, lo), vs, 1, 0)

    core_rs, x_rs, x_ag, core_ag = [], [], [], []
    theirs = projected(0, 1 - c)
    for h in range(2):
        part[h] = theirs[:, h * HALF : (h + 1) * HALF]
    pl.semaphore_wait(barrier, len(everyone))
    for h in range(2):
        core_rs.append(send(part.at[h], crecv.at[h], c_s.at[h, 0], c_r.at[h, 0], dev(z, y, x, 1 - c)))
    ours = projected(1, c)
    for h in range(2):
        core_rs[h].wait_recv()
        half[h] = ours[:, h * HALF : (h + 1) * HALF] + crecv[h]
        x_rs.append([
            send(half.at[h, ds(64 * peer_x(i), 64)], xrecv.at[h, i - 1], x_s.at[h, 0, i - 1], x_r.at[h, 0, i - 1],
                 dev(z, y, peer_x(i), c))
            for i in range(1, NX)
        ])
    for h in range(2):
        for cp in x_rs[h]:
            cp.wait_recv()
        total = half[h, ds(64 * x, 64), :]
        for i in range(NX - 1):
            total = total + xrecv[h, i]
        own[h] = total
        at = 256 * c + 64 * x
        x_ag.append([
            send(own.at[h], pfull.at[h, ds(at, 64)], x_s.at[h, 1, i - 1], x_r.at[h, 1, i - 1], dev(z, y, peer_x(i), c))
            for i in range(1, NX)
        ])
        core_ag.append([
            send(own.at[h], pfull.at[h, ds(at, 64)], c_s.at[h, 1], c_r.at[h, 1], dev(z, y, x, 1 - c))
        ])
        pfull[h, ds(at, 64), :] = total
    for h in range(2):
        for i in range(1, NX):
            x_ag[h][i - 1].wait_recv()
            at = 256 * c + 64 * lax.rem(x + NX - i, NX)
            core_ag[h].append(
                send(pfull.at[h, ds(at, 64)], pfull.at[h, ds(at, 64)], c_s.at[h, 1 + i], c_r.at[h, 1 + i],
                     dev(z, y, x, 1 - c))
            )
        for cp in core_ag[h]:
            cp.wait_recv()
        ph = pfull[h].T
        pt[h * HALF : (h + 1) * HALF, :] = ph
        if h == 0:
            w[:HALF, :] = dot3(split(ph), (bh[...], bl[...]), 1, 0)

    rows = ds(32 * ti, 32)
    ptr = pt[rows, :]
    for h in range(2):
        gpart[:, h * HALF : (h + 1) * HALF] = dot_f32(ptr, pfull[h], 1, 0)
    g1 = [
        send(gpart.at[ds(8 * peer_y(i), 8)], gyrecv.at[i - 1], g_s.at[0, i - 1], g_r.at[0, i - 1],
             dev(z, peer_y(i), x, c))
        for i in range(1, NY)
    ]
    w[HALF:, :] = dot3(split(ph), (bh[...], bl[...]), 1, 0)

    def to_y(i):
        return dev(z, peer_y(i), x, c)

    def to_z(i):
        return dev(peer_z(i), y, x, c)

    rs1, rs2, ag1, ag2 = {}, {}, {}, {}

    def start_rs1(n):
        c0, nc, first = CHUNKS[n]
        cs = pl.ds(c0, nc)
        if first == "y":
            rs1[n] = [
                send(w.at[ds(64 * peer_y(i), 64), cs], r1y.at[i - 1, :, cs], w_s.at[n, 0, i - 1], w_r.at[n, 0, i - 1], to_y(i))
                for i in range(1, NY)
            ]
        else:
            rs1[n] = [
                send(w.at[ds(32 * peer_z(i), 32), cs], r1z.at[i - 1, :, cs], w_s.at[n, 0, i - 1], w_r.at[n, 0, i - 1], to_z(i))
                for i in range(1, NZ)
            ]

    def start_rs2(n):
        c0, nc, first = CHUNKS[n]
        cs = pl.ds(c0, nc)
        for cp in rs1[n]:
            cp.wait_recv()
        if first == "y":
            total = w[ds(64 * y, 64), cs]
            for i in range(NY - 1):
                total = total + r1y[i, :, cs]
            s1y[:, cs] = total
            rs2[n] = [
                send(s1y.at[ds(8 * peer_z(i), 8), cs], r2z.at[i - 1, :, cs], w_s.at[n, 1, i - 1], w_r.at[n, 1, i - 1], to_z(i))
                for i in range(1, NZ)
            ]
        else:
            total = w[ds(32 * z, 32), cs]
            for i in range(NZ - 1):
                total = total + r1z[i, :, cs]
            s1z[:, cs] = total
            rs2[n] = [
                send(s1z.at[ds(8 * peer_y(i), 8), cs], r2y.at[i - 1, :, cs], w_s.at[n, 1, i - 1], w_r.at[n, 1, i - 1], to_y(i))
                for i in range(1, NY)
            ]

    def start_ag1(n):
        c0, nc, first = CHUNKS[n]
        cs = pl.ds(c0, nc)
        for cp in rs2[n]:
            cp.wait_recv()
        if first == "y":
            total = s1y[ds(8 * z, 8), cs]
            for i in range(NZ - 1):
                total = total + r2z[i, :, cs]
            at = 64 * y + 8 * z
            s2[:, cs] = total
            ag1[n] = [
                send(s2.at[:, cs], wf.at[ds(at, 8), cs], w_s.at[n, 2, i - 1], w_r.at[n, 2, i - 1], to_z(i))
                for i in range(1, NZ)
            ]
        else:
            total = s1z[ds(8 * y, 8), cs]
            for i in range(NY - 1):
                total = total + r2y[i, :, cs]
            at = 32 * z + 8 * y
            s2[:, cs] = total
            ag1[n] = [
                send(s2.at[:, cs], wf.at[ds(at, 8), cs], w_s.at[n, 2, i - 1], w_r.at[n, 2, i - 1], to_y(i))
                for i in range(1, NY)
            ]
        wf[ds(at, 8), cs] = total

    def start_ag2(n):
        c0, nc, first = CHUNKS[n]
        cs = pl.ds(c0, nc)
        for cp in ag1[n]:
            cp.wait_recv()
        if first == "y":
            piece = wf.at[ds(64 * y, 64), cs]
            ag2[n] = [
                send(piece, piece, w_s.at[n, 3, i - 1], w_r.at[n, 3, i - 1], to_y(i)) for i in range(1, NY)
            ]
        else:
            piece = wf.at[ds(32 * z, 32), cs]
            ag2[n] = [
                send(piece, piece, w_s.at[n, 3, i - 1], w_r.at[n, 3, i - 1], to_z(i)) for i in range(1, NZ)
            ]

    for n in range(len(CHUNKS)):
        start_rs1(n)
    for cp in g1:
        cp.wait_recv()
    total = gpart[ds(8 * y, 8), :]
    for i in range(NY - 1):
        total = total + gyrecv[i]
    gz[z] = total
    g2 = [send(gz.at[z], gz.at[z], g_s.at[1, i - 1], g_r.at[1, i - 1], to_z(i)) for i in range(1, NZ)]
    start_rs2(1)
    start_rs2(2)
    start_rs2(0)
    for cp in g2:
        cp.wait_recv()
    total = gz[0]
    for i in range(1, NZ):
        total = total + gz[i]
    mine = ds(32 * ti + 8 * y, 8)
    gmat[mine, :] = total
    g3 = [
        send(gmat.at[mine], gmat.at[mine], g_s.at[2 + i, j], g_r.at[2 + i, j], dev(z, peer_y(j), peer_x(i), c))
        for i in range(NX)
        for j in range(NY)
        if i or j
    ]
    start_rs2(3)
    start_ag1(1)
    start_ag1(0)
    start_ag1(2)
    g4 = []
    for i in range(NX):
        for j in range(NY):
            if i or j:
                g3[NY * i + j - 1].wait_recv()
        block = ds(64 * lax.rem(x + NX - i, NX) + 32 * c, 32)
        g4.append(send(gmat.at[block], gmat.at[block], g_s.at[6, i], g_r.at[6, i], dev(z, y, x, 1 - c)))
    start_ag1(3)
    for cp in g4:
        cp.wait_recv()
    for cp in g3 + g4:
        cp.wait_send()
    done = [id(cp) for cp in g3 + g4]
    pending[:] = [cp for cp in pending if id(cp) not in done]

    plan = {
        0: [(start_ag2, 0)],
        2: [(start_ag2, 1)],
        4: [(start_ag2, 2)],
        8: [(start_ag2, 3)],
    }
    panels = []

    def service():
        for step, n in plan.get(len(panels), ()):
            step(n)
        panels.append(0)

    cholesky_inverse(gmat, service)
    row = lax.broadcasted_iota(jnp.int32, (RANK, RANK), 0)
    lane = lax.broadcasted_iota(jnp.int32, (RANK, RANK), 1)
    inv = split(jnp.where(row >= lane, gmat[...], 0.0))
    q = dot3(split(pfull[0]), (inv[0][:, :HALF], inv[1][:, :HALF]), 1, 1)
    q = q + dot3(split(pfull[1]), (inv[0][:, HALF:], inv[1][:, HALF:]), 1, 1)
    for n in range(len(CHUNKS)):
        for cp in ag2[n]:
            cp.wait_recv()
    rt = dot3(inv, split(wf[...]), 1, 0)
    squares = rt[:, :128] * rt[:, :128]
    for k in range(1, BC // 128):
        piece = rt[:, k * 128 : (k + 1) * 128]
        squares = squares + piece * piece
    squares = squares.T
    total = squares[0:8, :]
    for k in range(1, 16):
        total = total + squares[8 * k : 8 * k + 8, :]
    nbuf[ti] = total
    n1 = [send(nbuf.at[ti], nbuf.at[ti], n_s.at[i], n_r.at[i], p) for i, p in enumerate(tensor_peers)]
    rsplit = split(rt)
    rh_ref[...], rl_ref[...] = rsplit
    for k in range(2):
        rows = ds(256 * (1 - c if k == 0 else c), 256)
        qk = jnp.where(c == k, q[256:], q[:256])
        nm_ref[rows, :] = mv[k] + gv[k].astype(F32) - dot3(split(0.5 * qk), rsplit, 1, 0)
    rtt_ref[...] = rt.T
    for cp in n1:
        cp.wait_recv()
    total = nbuf[0]
    for i in range(1, 2 * NX):
        total = total + nbuf[i]
    total = jnp.sum(total, axis=0, keepdims=True)
    scale = lax.rsqrt(total / COLS + 1e-06)
    norm_ref[...] = jnp.broadcast_to(scale, (8, RANK))
    q_ref[...] = q * (scale * (0.2 * math.sqrt(ROWS / RANK)))
    load_w.wait()
    for cp in pending:
        cp.wait_send()


def output_kernel(nm_ref, wv_ref, q_ref, rh_ref, rl_ref, rtt_ref, norm_ref, onm_ref, onw_ref, onr_ref, nw, nr, sems):
    copies = [pltpu.make_async_copy(nm_ref, onm_ref, sems.at[0])]
    copies[0].start()
    nr[...] = rtt_ref[...] * norm_ref[0:1, :]
    copies.append(pltpu.make_async_copy(nr, onr_ref, sems.at[1]))
    copies[1].start()
    right = (rh_ref[...], rl_ref[...])
    for k in range(2):
        rows = pl.ds(256 * k, 256)
        nw[rows, :] = wv_ref[rows, :] - dot3(split(q_ref[rows, :]), right, 1, 0)
        copies.append(pltpu.make_async_copy(nw.at[rows], onw_ref.at[rows], sems.at[2 + k]))
        copies[2 + k].start()
    for cp in copies:
        cp.wait()


def hbm(array):
    return pltpu.with_memory_space_constraint(array, pltpu.HBM)


def body(momentum, gradient, weights, prior_right):
    vmem = pl.BlockSpec(memory_space=pltpu.VMEM)
    nch = len(CHUNKS)
    dma = pltpu.SemaphoreType.DMA
    inner = (
        pltpu.VMEM((BR, BC), F32),
        pltpu.VMEM((BR, BC), F32),
        pltpu.VMEM((BR, RANK), F32),
        pltpu.VMEM((RANK, BC), BF16),
        pltpu.VMEM((RANK, BC), BF16),
        pltpu.VMEM((BC, RANK), F32),
        pltpu.VMEM((8, RANK), F32),
    )
    factors = pl.pallas_call(
        factor_kernel,
        out_shape=inner,
        in_specs=[pl.BlockSpec(memory_space=pltpu.HBM)] * 4,
        out_specs=(vmem,) * len(inner),
        scratch_shapes=[
            pltpu.VMEM((2, 256, BC), F32),
            pltpu.VMEM((2, 256, BC), BF16),
            pltpu.VMEM((BC, RANK), F32),
            pltpu.VMEM((BR, BC), BF16),
            pltpu.VMEM((BR, BC), BF16),
            pltpu.VMEM((2, 256, HALF), F32),
            pltpu.VMEM((2, 256, HALF), F32),
            pltpu.VMEM((2, 256, HALF), F32),
            pltpu.VMEM((2, NX - 1, 64, HALF), F32),
            pltpu.VMEM((2, 64, HALF), F32),
            pltpu.VMEM((2, BR, HALF), F32),
            pltpu.VMEM((RANK, BR), F32),
            pltpu.VMEM((32, RANK), F32),
            pltpu.VMEM((NY - 1, 8, RANK), F32),
            pltpu.VMEM((NZ, 8, RANK), F32),
            pltpu.VMEM((RANK, RANK), F32),
            pltpu.VMEM((RANK, BC), F32),
            pltpu.VMEM((RANK, BC), F32),
            pltpu.VMEM((NY - 1, 64, BC), F32),
            pltpu.VMEM((NZ - 1, 32, BC), F32),
            pltpu.VMEM((64, BC), F32),
            pltpu.VMEM((32, BC), F32),
            pltpu.VMEM((NY - 1, 8, BC), F32),
            pltpu.VMEM((NZ - 1, 8, BC), F32),
            pltpu.VMEM((8, BC), F32),
            pltpu.VMEM((2 * NX, 8, RANK), F32),
            dma((6,)),
            dma((2, 5)), dma((2, 5)),
            dma((2, 2, 3)), dma((2, 2, 3)),
            dma((7, 7)), dma((7, 7)),
            dma((nch, 4, 7)), dma((nch, 4, 7)),
            dma((7,)), dma((7,)),
        ],
        compiler_params=pltpu.CompilerParams(
            collective_id=0, has_side_effects=True, vmem_limit_bytes=40 * 1024 * 1024
        ),
        name="factors",
    )(hbm(momentum), hbm(gradient), hbm(weights), hbm(prior_right))
    return pl.pallas_call(
        output_kernel,
        out_shape=(
            jax.ShapeDtypeStruct((BR, BC), F32),
            jax.ShapeDtypeStruct((BR, BC), F32),
            jax.ShapeDtypeStruct((BC, RANK), F32),
        ),
        in_specs=[vmem] * len(inner),
        out_specs=(pl.BlockSpec(memory_space=pltpu.HBM),) * 3,
        scratch_shapes=[pltpu.VMEM((BR, BC), F32), pltpu.VMEM((BC, RANK), F32), dma((4,))],
        compiler_params=pltpu.CompilerParams(vmem_limit_bytes=40 * 1024 * 1024),
        name="outputs",
    )(*[pltpu.with_memory_space_constraint(a, pltpu.VMEM) for a in factors])


def solution(mesh):
    in_specs = (P("fsdp", "tensor"), P("fsdp", "tensor"), P("fsdp", "tensor"), P("tensor", None))
    out_specs = (P("fsdp", "tensor"), P("fsdp", "tensor"), P("tensor", None))
    return jax.shard_map(body, mesh=mesh, in_specs=in_specs, out_specs=out_specs, check_vma=False)
```

```python
import functools
import math

import jax
import jax.numpy as jnp
from jax import lax
from jax.experimental import pallas as pl
from jax.experimental.pallas import tpu as pltpu
from jax.sharding import PartitionSpec as P

ROWS = 16384
COLS = 9216
RANK = 256
NZ, NY, NX = 8, 4, 4
BR = 512
BC = 1152
HALF = 128
LEAF = 64
PANEL = 16
F32 = jnp.float32
BF16 = jnp.bfloat16
MESH = pl.DeviceIdType.MESH
CHUNKS = ((0, 256, "z"), (256, 128, "y"), (384, 256, "y"), (640, 256, "y"), (896, 256, "y"))


def dot_f32(a, b, ca, cb):
    return lax.dot_general(
        a, b, (((ca,), (cb,)), ((), ())), precision=lax.Precision.HIGHEST, preferred_element_type=F32
    )


def split(a):
    hi = a.astype(BF16)
    return hi, (a - hi.astype(F32)).astype(BF16)


def dot_bf16(a, b, ca, cb):
    return lax.dot_general(a, b, (((ca,), (cb,)), ((), ())), preferred_element_type=F32)


def dot3(a, b, ca, cb):
    return dot_bf16(
        jnp.concatenate([a[0], a[0], a[1]], axis=ca), jnp.concatenate([b[1], b[0], b[0]], axis=cb), ca, cb
    )


def leaf_elimination(block, service):
    n = block.shape[0]
    row = lax.broadcasted_iota(jnp.int32, (n, n), 0)
    lane = lax.broadcasted_iota(jnp.int32, (n, n), 1)
    for p0 in range(0, n, PANEL):
        cols = [jnp.broadcast_to(block[p0:, p0 + j : p0 + j + 1], (n - p0, n)) for j in range(PANEL)]
        rw, ln, low = row[p0:], lane[p0:], block[p0:]
        for k in range(PANEL):
            r = 1.0 / cols[k][k : k + 1, :]
            f = jnp.where(rw > p0 + k, cols[k] * r, 0.0)
            for j in range(k + 1, PANEL):
                cols[j] = cols[j] - f * cols[j][k : k + 1, :]
            pivot_row = jnp.where(ln[0:1] == p0 + k, 1.0, low[k : k + 1, :])
            cleared = jnp.where((ln == p0 + k) & (rw > p0 + k), 0.0, low)
            low = cleared - f * pivot_row
        block = jnp.concatenate([block[:p0], low], axis=0) if p0 else low
        service()
    return block


def cholesky_inverse(a, service):
    blocks = RANK // LEAF
    for j in range(blocks):
        s = slice(j * LEAF, (j + 1) * LEAF)
        d = leaf_elimination(a[s, s], service)
        row = lax.broadcasted_iota(jnp.int32, (LEAF, LEAF), 0)
        lane = lax.broadcasted_iota(jnp.int32, (LEAF, LEAF), 1)
        pivot = jnp.sum(jnp.where(row == lane, d, 0.0), axis=1, keepdims=True)
        unit = jnp.where(row > lane, d, jnp.where(row == lane, 1.0, 0.0))
        inv = unit * lax.rsqrt(pivot)
        x = dot_f32(inv, a[s, :], 1, 0)
        a[s, :] = x
        a[s, s] = inv
        if j < blocks - 1:
            low = (j + 1) * LEAF
            a[low:, s] = jnp.zeros((RANK - low, LEAF), F32)
            a[low:, :] = a[low:, :] - dot_f32(x[:, low:], a[s, :], 0, 0)


def factor_kernel(
    m_ref, g_ref, wt_ref, v_ref, nm_ref, wv_ref, q_ref, rh_ref, rl_ref, rtt_ref, norm_ref,
    mv, gv, vv, bh, bl, part, crecv, half, xrecv, own, pfull, pt,
    gpart, gyrecv, gz, gsum, gmat,
    w, wf, r1y, r1z, s1y, s1z, r2y, r2z, s2,
    nbuf, l_s, c_s, c_r, x_s, x_r, g_s, g_r, w_s, w_r, n_s, n_r,
):
    fi, ti = lax.axis_index("fsdp"), lax.axis_index("tensor")
    z, y = fi // NY, lax.rem(fi, NY)
    x, c = ti // 2, lax.rem(ti, 2)

    def dev(zz, yy, xx, cc):
        return (zz * NY + yy, xx * 2 + cc)

    def peer_z(i):
        return lax.rem(z + i, NZ)

    def peer_y(i):
        return lax.rem(y + i, NY)

    def peer_x(i):
        return lax.rem(x + i, NX)

    def ds(start, size):
        return pl.ds(pl.multiple_of(start, size if size < 16 else 16), size)

    pending = []

    def send(copies, sems, size):
        for src, dst, to in copies:
            pltpu.make_async_remote_copy(
                src_ref=src, dst_ref=dst, send_sem=sems[0], recv_sem=sems[1], device_id=to, device_id_type=MESH
            ).start()
        group = pltpu.make_async_remote_copy(
            src_ref=size, dst_ref=size, send_sem=sems[0], recv_sem=sems[1], device_id=copies[0][2], device_id_type=MESH
        )
        pending.append(group)
        return group

    def both(sem_s, sem_r, *at):
        return sem_s.at[at], sem_r.at[at]

    load_v = pltpu.make_async_copy(v_ref, vv, l_s.at[0])
    load_v.start()
    loads = []
    for k, cc in enumerate((1 - c, c)):
        rows = ds(256 * cc, 256)
        loads.append([
            pltpu.make_async_copy(m_ref.at[rows], mv.at[k], l_s.at[1 + 2 * k]),
            pltpu.make_async_copy(g_ref.at[rows], gv.at[k], l_s.at[2 + 2 * k]),
        ])
        for cp in loads[k]:
            cp.start()

    barrier = pltpu.get_barrier_semaphore()
    peers = [dev(z, peer_y(i), x, c) for i in range(1, NY)]
    peers += [dev(peer_z(i), y, x, c) for i in range(1, NZ)]
    tensor_peers = [dev(z, y, x, 1 - c)]
    tensor_peers += [dev(z, y, peer_x(i), cc) for i in range(1, NX) for cc in (c, 1 - c)]
    plane_peers = [dev(z, peer_y(j), peer_x(i), c) for i in range(1, NX) for j in range(1, NY)]
    everyone = peers + tensor_peers + plane_peers
    for p in everyone:
        pl.semaphore_signal(barrier, inc=1, device_id=p, device_id_type=MESH)

    load_v.wait()
    vs = split(vv[...])

    def projected(k, cc):
        for cp in loads[k]:
            cp.wait()
        rows = ds(256 * cc, 256)
        hi, lo = split(mv[k] + gv[k].astype(F32))
        bh[rows, :] = hi
        bl[rows, :] = lo
        return dot3((hi, lo), vs, 1, 0)

    other = dev(z, y, x, 1 - c)
    x_peers = [(i, dev(z, y, peer_x(i), c)) for i in range(1, NX)]
    core_rs, x_rs, x_ag = [], [], []
    theirs = projected(0, 1 - c)
    for h in range(2):
        part[h] = theirs[:, h * HALF : (h + 1) * HALF]
    pl.semaphore_wait(barrier, len(everyone))
    for h in range(2):
        core_rs.append(send([(part.at[h], crecv.at[h], other)], both(c_s, c_r, h, 0), crecv.at[h]))
    ours = projected(1, c)
    load_w = pltpu.make_async_copy(wt_ref, wv_ref, l_s.at[5])
    load_w.start()
    for h in range(2):
        core_rs[h].wait_recv()
        half[h] = ours[:, h * HALF : (h + 1) * HALF] + crecv[h]
        x_rs.append(send(
            [(half.at[h, ds(64 * peer_x(i), 64)], xrecv.at[h, i - 1], to) for i, to in x_peers],
            both(x_s, x_r, h, 0), xrecv.at[h],
        ))
    for h in range(2):
        x_rs[h].wait_recv()
        total = half[h, ds(64 * x, 64), :]
        for i in range(NX - 1):
            total = total + xrecv[h, i]
        own[h] = total
        piece = pfull.at[h, ds(256 * c + 64 * x, 64)]
        x_ag.append(send([(own.at[h], piece, to) for _, to in x_peers], both(x_s, x_r, h, 1), xrecv.at[h]))
        pfull[h, ds(256 * c + 64 * x, 64), :] = total
    for h in range(2):
        x_ag[h].wait_recv()
        piece = pfull.at[h, ds(256 * c, 256)]
        send([(piece, piece, other)], both(c_s, c_r, h, 1), piece).wait_recv()
        ph = pfull[h].T
        pt[h * HALF : (h + 1) * HALF, :] = ph
        if h == 0:
            w[:HALF, :] = dot3(split(ph), (bh[...], bl[...]), 1, 0)

    rows = ds(32 * ti, 32)
    ptr = pt[rows, :]
    for h in range(2):
        gpart[:, h * HALF : (h + 1) * HALF] = dot_f32(ptr, pfull[h], 1, 0)
    g1 = send(
        [(gpart.at[ds(8 * peer_y(i), 8)], gyrecv.at[i - 1], dev(z, peer_y(i), x, c)) for i in range(1, NY)],
        both(g_s, g_r, 0), gyrecv,
    )
    w[HALF:, :] = dot3(split(ph), (bh[...], bl[...]), 1, 0)

    y_peers = [(i, dev(z, peer_y(i), x, c)) for i in range(1, NY)]
    z_peers = [(i, dev(peer_z(i), y, x, c)) for i in range(1, NZ)]
    rs1, rs2, ag1, ag2 = {}, {}, {}, {}

    def start_rs1(n):
        c0, nc, first = CHUNKS[n]
        cs = pl.ds(c0, nc)
        sems = both(w_s, w_r, n, 0)
        if first == "y":
            rs1[n] = send(
                [(w.at[ds(64 * peer_y(i), 64), cs], r1y.at[i - 1, :, cs], to) for i, to in y_peers], sems, r1y.at[:, :, cs]
            )
        else:
            rs1[n] = send(
                [(w.at[ds(32 * peer_z(i), 32), cs], r1z.at[i - 1, :, cs], to) for i, to in z_peers], sems, r1z.at[:, :, cs]
            )

    def start_rs2(n):
        c0, nc, first = CHUNKS[n]
        cs = pl.ds(c0, nc)
        sems = both(w_s, w_r, n, 1)
        rs1[n].wait_recv()
        if first == "y":
            total = w[ds(64 * y, 64), cs]
            for i in range(NY - 1):
                total = total + r1y[i, :, cs]
            s1y[:, cs] = total
            rs2[n] = send(
                [(s1y.at[ds(8 * peer_z(i), 8), cs], r2z.at[i - 1, :, cs], to) for i, to in z_peers], sems, r2z.at[:, :, cs]
            )
        else:
            total = w[ds(32 * z, 32), cs]
            for i in range(NZ - 1):
                total = total + r1z[i, :, cs]
            s1z[:, cs] = total
            rs2[n] = send(
                [(s1z.at[ds(8 * peer_y(i), 8), cs], r2y.at[i - 1, :, cs], to) for i, to in y_peers], sems, r2y.at[:, :, cs]
            )

    def start_ag1(n):
        c0, nc, first = CHUNKS[n]
        cs = pl.ds(c0, nc)
        sems = both(w_s, w_r, n, 2)
        rs2[n].wait_recv()
        if first == "y":
            total = s1y[ds(8 * z, 8), cs]
            for i in range(NZ - 1):
                total = total + r2z[i, :, cs]
            piece, to_all, size = wf.at[ds(64 * y + 8 * z, 8), cs], z_peers, r2z.at[:, :, cs]
        else:
            total = s1z[ds(8 * y, 8), cs]
            for i in range(NY - 1):
                total = total + r2y[i, :, cs]
            piece, to_all, size = wf.at[ds(32 * z + 8 * y, 8), cs], y_peers, r2y.at[:, :, cs]
        s2[:, cs] = total
        ag1[n] = send([(s2.at[:, cs], piece, to) for _, to in to_all], sems, size)
        piece[...] = total

    def start_ag2(n):
        c0, nc, first = CHUNKS[n]
        cs = pl.ds(c0, nc)
        sems = both(w_s, w_r, n, 3)
        ag1[n].wait_recv()
        if first == "y":
            piece, to_all, size = wf.at[ds(64 * y, 64), cs], y_peers, r1y.at[:, :, cs]
        else:
            piece, to_all, size = wf.at[ds(32 * z, 32), cs], z_peers, r1z.at[:, :, cs]
        ag2[n] = send([(piece, piece, to) for _, to in to_all], sems, size)

    for n in range(len(CHUNKS)):
        start_rs1(n)
    g1.wait_recv()
    total = gpart[ds(8 * y, 8), :]
    for i in range(NY - 1):
        total = total + gyrecv[i]
    gz[z] = total
    g2 = send([(gz.at[z], gz.at[z], to) for _, to in z_peers], both(g_s, g_r, 1), gz.at[pl.ds(0, NZ - 1)])
    start_rs2(1)
    start_rs2(2)
    start_rs2(3)
    start_rs2(0)
    g2.wait_recv()
    total = gz[0]
    for i in range(1, NZ):
        total = total + gz[i]
    mine = gsum.at[x, c, ds(8 * y, 8)]
    mine[...] = total
    g3 = send(
        [(mine, mine, dev(z, peer_y(j), peer_x(i), c)) for i in range(NX) for j in range(NY) if i or j],
        both(g_s, g_r, 2), w.at[pl.ds(0, 8 * (NX * NY - 1)), pl.ds(0, RANK)],
    )
    start_ag1(1)
    start_rs2(4)
    start_ag1(0)
    start_ag1(2)
    g3.wait_recv()
    ours = gsum.at[:, c]
    g4 = send([(ours, ours, other)], both(g_s, g_r, 3), ours)
    start_ag1(3)
    start_ag2(1)
    start_ag2(0)
    start_ag1(4)
    g4.wait_recv()
    for i in range(NX):
        for k in range(2):
            gmat[64 * i + 32 * k : 64 * i + 32 * k + 32, :] = gsum[i, k]

    plan = {
        2: [(start_ag2, 2)],
        5: [(start_ag2, 3)],
        9: [(start_ag2, 4)],
    }
    panels = []

    def service():
        for step, n in plan.get(len(panels), ()):
            step(n)
        panels.append(0)

    cholesky_inverse(gmat, service)
    row = lax.broadcasted_iota(jnp.int32, (RANK, RANK), 0)
    lane = lax.broadcasted_iota(jnp.int32, (RANK, RANK), 1)
    inv = split(jnp.where(row >= lane, gmat[...], 0.0))
    q = dot3(split(pfull[0]), (inv[0][:, :HALF], inv[1][:, :HALF]), 1, 1)
    q = q + dot3(split(pfull[1]), (inv[0][:, HALF:], inv[1][:, HALF:]), 1, 1)
    for n in range(len(CHUNKS)):
        ag2[n].wait_recv()
    rt = dot3(inv, split(wf[...]), 1, 0)
    squares = rt[:, :128] * rt[:, :128]
    for k in range(1, BC // 128):
        piece = rt[:, k * 128 : (k + 1) * 128]
        squares = squares + piece * piece
    squares = squares.T
    total = squares[0:8, :]
    for k in range(1, 16):
        total = total + squares[8 * k : 8 * k + 8, :]
    nbuf[ti] = total
    n1 = send([(nbuf.at[ti], nbuf.at[ti], p) for p in tensor_peers], both(n_s, n_r, 0), nbuf.at[pl.ds(0, 2 * NX - 1)])
    rsplit = split(rt)
    rh_ref[...], rl_ref[...] = rsplit
    for k in range(2):
        rows = ds(256 * (1 - c if k == 0 else c), 256)
        qk = jnp.where(c == k, q[256:], q[:256])
        nm_ref[rows, :] = mv[k] + gv[k].astype(F32) - dot3(split(0.5 * qk), rsplit, 1, 0)
    rtt_ref[...] = rt.T
    n1.wait_recv()
    total = nbuf[0]
    for i in range(1, 2 * NX):
        total = total + nbuf[i]
    total = jnp.sum(total, axis=0, keepdims=True)
    scale = lax.rsqrt(total / COLS + 1e-06)
    norm_ref[...] = jnp.broadcast_to(scale, (8, RANK))
    q_ref[...] = q * (scale * (0.2 * math.sqrt(ROWS / RANK)))
    load_w.wait()
    for cp in pending:
        cp.wait_send()


def output_kernel(nm_ref, wv_ref, q_ref, rh_ref, rl_ref, rtt_ref, norm_ref, onm_ref, onw_ref, onr_ref, nw, nr, sems):
    copies = [pltpu.make_async_copy(nm_ref, onm_ref, sems.at[0])]
    copies[0].start()
    nr[...] = rtt_ref[...] * norm_ref[0:1, :]
    copies.append(pltpu.make_async_copy(nr, onr_ref, sems.at[1]))
    copies[1].start()
    right = (rh_ref[...], rl_ref[...])
    for k in range(2):
        rows = pl.ds(256 * k, 256)
        nw[rows, :] = wv_ref[rows, :] - dot3(split(q_ref[rows, :]), right, 1, 0)
        copies.append(pltpu.make_async_copy(nw.at[rows], onw_ref.at[rows], sems.at[2 + k]))
        copies[2 + k].start()
    for cp in copies:
        cp.wait()


def hbm(array):
    return pltpu.with_memory_space_constraint(array, pltpu.HBM)


def body(momentum, gradient, weights, prior_right):
    vmem = pl.BlockSpec(memory_space=pltpu.VMEM)
    dma = pltpu.SemaphoreType.DMA
    inner = (
        pltpu.VMEM((BR, BC), F32),
        pltpu.VMEM((BR, BC), F32),
        pltpu.VMEM((BR, RANK), F32),
        pltpu.VMEM((RANK, BC), BF16),
        pltpu.VMEM((RANK, BC), BF16),
        pltpu.VMEM((BC, RANK), F32),
        pltpu.VMEM((8, RANK), F32),
    )
    factors = pl.pallas_call(
        factor_kernel,
        out_shape=inner,
        in_specs=[pl.BlockSpec(memory_space=pltpu.HBM)] * 4,
        out_specs=(vmem,) * len(inner),
        scratch_shapes=[
            pltpu.VMEM((2, 256, BC), F32),
            pltpu.VMEM((2, 256, BC), BF16),
            pltpu.VMEM((BC, RANK), F32),
            pltpu.VMEM((BR, BC), BF16),
            pltpu.VMEM((BR, BC), BF16),
            pltpu.VMEM((2, 256, HALF), F32),
            pltpu.VMEM((2, 256, HALF), F32),
            pltpu.VMEM((2, 256, HALF), F32),
            pltpu.VMEM((2, NX - 1, 64, HALF), F32),
            pltpu.VMEM((2, 64, HALF), F32),
            pltpu.VMEM((2, BR, HALF), F32),
            pltpu.VMEM((RANK, BR), F32),
            pltpu.VMEM((32, RANK), F32),
            pltpu.VMEM((NY - 1, 8, RANK), F32),
            pltpu.VMEM((NZ, 8, RANK), F32),
            pltpu.VMEM((NX, 2, 32, RANK), F32),
            pltpu.VMEM((RANK, RANK), F32),
            pltpu.VMEM((RANK, BC), F32),
            pltpu.VMEM((RANK, BC), F32),
            pltpu.VMEM((NY - 1, 64, BC), F32),
            pltpu.VMEM((NZ - 1, 32, BC), F32),
            pltpu.VMEM((64, BC), F32),
            pltpu.VMEM((32, BC), F32),
            pltpu.VMEM((NY - 1, 8, BC), F32),
            pltpu.VMEM((NZ - 1, 8, BC), F32),
            pltpu.VMEM((8, BC), F32),
            pltpu.VMEM((2 * NX, 8, RANK), F32),
            dma((6,)),
            dma((2, 2)), dma((2, 2)),
            dma((2, 2)), dma((2, 2)),
            dma((4,)), dma((4,)),
            dma((len(CHUNKS), 4)), dma((len(CHUNKS), 4)),
            dma((1,)), dma((1,)),
        ],
        compiler_params=pltpu.CompilerParams(
            collective_id=0, has_side_effects=True, vmem_limit_bytes=40 * 1024 * 1024
        ),
        name="factors",
    )(hbm(momentum), hbm(gradient), hbm(weights), hbm(prior_right))
    return pl.pallas_call(
        output_kernel,
        out_shape=(
            jax.ShapeDtypeStruct((BR, BC), F32),
            jax.ShapeDtypeStruct((BR, BC), F32),
            jax.ShapeDtypeStruct((BC, RANK), F32),
        ),
        in_specs=[vmem] * len(inner),
        out_specs=(pl.BlockSpec(memory_space=pltpu.HBM),) * 3,
        scratch_shapes=[pltpu.VMEM((BR, BC), F32), pltpu.VMEM((BC, RANK), F32), dma((4,))],
        compiler_params=pltpu.CompilerParams(vmem_limit_bytes=40 * 1024 * 1024),
        name="outputs",
    )(*[pltpu.with_memory_space_constraint(a, pltpu.VMEM) for a in factors])


def solution(mesh):
    in_specs = (P("fsdp", "tensor"), P("fsdp", "tensor"), P("fsdp", "tensor"), P("tensor", None))
    out_specs = (P("fsdp", "tensor"), P("fsdp", "tensor"), P("tensor", None))
    return jax.shard_map(body, mesh=mesh, in_specs=in_specs, out_specs=out_specs, check_vma=False)
```

```python
import functools
import math

import jax
import jax.numpy as jnp
from jax import lax
from jax.experimental import pallas as pl
from jax.experimental.pallas import tpu as pltpu
from jax.sharding import PartitionSpec as P

ROWS = 16384
COLS = 9216
RANK = 256
NZ, NY, NX = 8, 4, 4
BR = 512
BC = 1152
HALF = 128
LEAF = 64
PANEL = 16
F32 = jnp.float32
BF16 = jnp.bfloat16
MESH = pl.DeviceIdType.MESH
CHUNKS = ((0, 256, "z"), (256, 256, "y"), (512, 256, "y"), (768, 256, "y"), (1024, 128, "y"))


def dot_f32(a, b, ca, cb):
    return lax.dot_general(
        a, b, (((ca,), (cb,)), ((), ())), precision=lax.Precision.HIGHEST, preferred_element_type=F32
    )


def split(a):
    hi = a.astype(BF16)
    return hi, (a - hi.astype(F32)).astype(BF16)


def dot_bf16(a, b, ca, cb):
    return lax.dot_general(a, b, (((ca,), (cb,)), ((), ())), preferred_element_type=F32)


def dot3(a, b, ca, cb):
    return dot_bf16(
        jnp.concatenate([a[0], a[0], a[1]], axis=ca), jnp.concatenate([b[1], b[0], b[0]], axis=cb), ca, cb
    )


def leaf_elimination(block, service):
    n = block.shape[0]
    row = lax.broadcasted_iota(jnp.int32, (n, n), 0)
    lane = lax.broadcasted_iota(jnp.int32, (n, n), 1)
    for p0 in range(0, n, PANEL):
        cols = [jnp.broadcast_to(block[p0:, p0 + j : p0 + j + 1], (n - p0, n)) for j in range(PANEL)]
        rw, ln, low = row[p0:], lane[p0:], block[p0:]
        for k in range(PANEL):
            r = 1.0 / cols[k][k : k + 1, :]
            below = jnp.where(rw > p0 + k, cols[k], 0.0)
            for j in range(k + 1, PANEL):
                cols[j] = cols[j] - below * (cols[j][k : k + 1, :] * r)
            pivot_row = jnp.where(ln[0:1] == p0 + k, 1.0, low[k : k + 1, :]) * r
            cleared = jnp.where((ln == p0 + k) & (rw > p0 + k), 0.0, low)
            low = cleared - below * pivot_row
        block = jnp.concatenate([block[:p0], low], axis=0) if p0 else low
        service()
    return block


def cholesky_inverse(a, service):
    blocks = RANK // LEAF
    for j in range(blocks):
        s = slice(j * LEAF, (j + 1) * LEAF)
        d = leaf_elimination(a[s, s], service)
        row = lax.broadcasted_iota(jnp.int32, (LEAF, LEAF), 0)
        lane = lax.broadcasted_iota(jnp.int32, (LEAF, LEAF), 1)
        pivot = jnp.sum(jnp.where(row == lane, d, 0.0), axis=1, keepdims=True)
        unit = jnp.where(row > lane, d, jnp.where(row == lane, 1.0, 0.0))
        inv = unit * lax.rsqrt(pivot)
        x = dot_f32(inv, a[s, :], 1, 0)
        a[s, :] = x
        a[s, s] = inv
        if j < blocks - 1:
            low = (j + 1) * LEAF
            a[low:, s] = jnp.zeros((RANK - low, LEAF), F32)
            a[low:, :] = a[low:, :] - dot_f32(x[:, low:], a[s, :], 0, 0)


def factor_kernel(
    m_ref, g_ref, wt_ref, v_ref, nm_ref, wv_ref, q_ref, rh_ref, rl_ref, rtt_ref, norm_ref,
    mv, gv, vv, bh, bl, part, crecv, half, xrecv, own, pfull, pt,
    gpart, gyrecv, gz, gsum, gmat,
    w, wf, r1y, r1z, s1y, s1z, r2y, r2z, s2,
    nbuf, l_s, c_s, c_r, x_s, x_r, g_s, g_r, w_s, w_r, n_s, n_r,
):
    fi, ti = lax.axis_index("fsdp"), lax.axis_index("tensor")
    z, y = fi // NY, lax.rem(fi, NY)
    x, c = ti // 2, lax.rem(ti, 2)

    def dev(zz, yy, xx, cc):
        return (zz * NY + yy, xx * 2 + cc)

    def peer_z(i):
        return lax.rem(z + i, NZ)

    def peer_y(i):
        return lax.rem(y + i, NY)

    def peer_x(i):
        return lax.rem(x + i, NX)

    def ds(start, size):
        return pl.ds(pl.multiple_of(start, size if size < 16 else 16), size)

    pending = []

    def send(copies, sems, size):
        for src, dst, to in copies:
            pltpu.make_async_remote_copy(
                src_ref=src, dst_ref=dst, send_sem=sems[0], recv_sem=sems[1], device_id=to, device_id_type=MESH
            ).start()
        group = pltpu.make_async_remote_copy(
            src_ref=size, dst_ref=size, send_sem=sems[0], recv_sem=sems[1], device_id=copies[0][2], device_id_type=MESH
        )
        pending.append(group)
        return group

    def both(sem_s, sem_r, *at):
        return sem_s.at[at], sem_r.at[at]

    load_v = pltpu.make_async_copy(v_ref, vv, l_s.at[0])
    load_v.start()
    loads = []
    for k, cc in enumerate((1 - c, c)):
        rows = ds(256 * cc, 256)
        loads.append([
            pltpu.make_async_copy(m_ref.at[rows], mv.at[k], l_s.at[1 + 2 * k]),
            pltpu.make_async_copy(g_ref.at[rows], gv.at[k], l_s.at[2 + 2 * k]),
        ])
        for cp in loads[k]:
            cp.start()

    barrier = pltpu.get_barrier_semaphore()
    peers = [dev(z, peer_y(i), x, c) for i in range(1, NY)]
    peers += [dev(peer_z(i), y, x, c) for i in range(1, NZ)]
    tensor_peers = [dev(z, y, x, 1 - c)]
    tensor_peers += [dev(z, y, peer_x(i), cc) for i in range(1, NX) for cc in (c, 1 - c)]
    plane_peers = [dev(z, peer_y(j), peer_x(i), c) for i in range(1, NX) for j in range(1, NY)]
    everyone = peers + tensor_peers + plane_peers
    for p in everyone:
        pl.semaphore_signal(barrier, inc=1, device_id=p, device_id_type=MESH)

    load_v.wait()
    vs = split(vv[...])

    def projected(k, cc):
        for cp in loads[k]:
            cp.wait()
        rows = ds(256 * cc, 256)
        hi, lo = split(mv[k] + gv[k].astype(F32))
        bh[rows, :] = hi
        bl[rows, :] = lo
        return dot3((hi, lo), vs, 1, 0)

    other = dev(z, y, x, 1 - c)
    x_peers = [(i, dev(z, y, peer_x(i), c)) for i in range(1, NX)]
    core_rs, x_rs, x_ag = [], [], []
    theirs = projected(0, 1 - c)
    for h in range(2):
        part[h] = theirs[:, h * HALF : (h + 1) * HALF]
    pl.semaphore_wait(barrier, len(everyone))
    for h in range(2):
        core_rs.append(send([(part.at[h], crecv.at[h], other)], both(c_s, c_r, h, 0), crecv.at[h]))
    ours = projected(1, c)
    load_w = pltpu.make_async_copy(wt_ref, wv_ref, l_s.at[5])
    load_w.start()
    for h in range(2):
        core_rs[h].wait_recv()
        half[h] = ours[:, h * HALF : (h + 1) * HALF] + crecv[h]
        x_rs.append(send(
            [(half.at[h, ds(64 * peer_x(i), 64)], xrecv.at[h, i - 1], to) for i, to in x_peers],
            both(x_s, x_r, h, 0), xrecv.at[h],
        ))
    for h in range(2):
        x_rs[h].wait_recv()
        total = half[h, ds(64 * x, 64), :]
        for i in range(NX - 1):
            total = total + xrecv[h, i]
        own[h] = total
        piece = pfull.at[h, ds(256 * c + 64 * x, 64)]
        x_ag.append(send([(own.at[h], piece, to) for _, to in x_peers], both(x_s, x_r, h, 1), xrecv.at[h]))
        pfull[h, ds(256 * c + 64 * x, 64), :] = total
    for h in range(2):
        x_ag[h].wait_recv()
        piece = pfull.at[h, ds(256 * c, 256)]
        send([(piece, piece, other)], both(c_s, c_r, h, 1), piece).wait_recv()
        ph = pfull[h].T
        pt[h * HALF : (h + 1) * HALF, :] = ph
        if h == 0:
            w[:HALF, :] = dot3(split(ph), (bh[...], bl[...]), 1, 0)

    rows = ds(32 * ti, 32)
    ptr = pt[rows, :]
    for h in range(2):
        gpart[:, h * HALF : (h + 1) * HALF] = dot_f32(ptr, pfull[h], 1, 0)
    g1 = send(
        [(gpart.at[ds(8 * peer_y(i), 8)], gyrecv.at[i - 1], dev(z, peer_y(i), x, c)) for i in range(1, NY)],
        both(g_s, g_r, 0), gyrecv,
    )
    w[HALF:, :] = dot3(split(ph), (bh[...], bl[...]), 1, 0)

    y_peers = [(i, dev(z, peer_y(i), x, c)) for i in range(1, NY)]
    z_peers = [(i, dev(peer_z(i), y, x, c)) for i in range(1, NZ)]
    rs1, rs2, ag1, ag2 = {}, {}, {}, {}

    def start_rs1(n):
        c0, nc, first = CHUNKS[n]
        cs = pl.ds(c0, nc)
        sems = both(w_s, w_r, n, 0)
        if first == "y":
            rs1[n] = send(
                [(w.at[ds(64 * peer_y(i), 64), cs], r1y.at[i - 1, :, cs], to) for i, to in y_peers], sems, r1y.at[:, :, cs]
            )
        else:
            rs1[n] = send(
                [(w.at[ds(32 * peer_z(i), 32), cs], r1z.at[i - 1, :, cs], to) for i, to in z_peers], sems, r1z.at[:, :, cs]
            )

    def start_rs2(n):
        c0, nc, first = CHUNKS[n]
        cs = pl.ds(c0, nc)
        sems = both(w_s, w_r, n, 1)
        rs1[n].wait_recv()
        if first == "y":
            total = w[ds(64 * y, 64), cs]
            for i in range(NY - 1):
                total = total + r1y[i, :, cs]
            s1y[:, cs] = total
            rs2[n] = send(
                [(s1y.at[ds(8 * peer_z(i), 8), cs], r2z.at[i - 1, :, cs], to) for i, to in z_peers], sems, r2z.at[:, :, cs]
            )
        else:
            total = w[ds(32 * z, 32), cs]
            for i in range(NZ - 1):
                total = total + r1z[i, :, cs]
            s1z[:, cs] = total
            rs2[n] = send(
                [(s1z.at[ds(8 * peer_y(i), 8), cs], r2y.at[i - 1, :, cs], to) for i, to in y_peers], sems, r2y.at[:, :, cs]
            )

    def start_ag1(n):
        c0, nc, first = CHUNKS[n]
        cs = pl.ds(c0, nc)
        sems = both(w_s, w_r, n, 2)
        rs2[n].wait_recv()
        if first == "y":
            total = s1y[ds(8 * z, 8), cs]
            for i in range(NZ - 1):
                total = total + r2z[i, :, cs]
            piece, to_all, size = wf.at[ds(64 * y + 8 * z, 8), cs], z_peers, r2z.at[:, :, cs]
        else:
            total = s1z[ds(8 * y, 8), cs]
            for i in range(NY - 1):
                total = total + r2y[i, :, cs]
            piece, to_all, size = wf.at[ds(32 * z + 8 * y, 8), cs], y_peers, r2y.at[:, :, cs]
        s2[:, cs] = total
        ag1[n] = send([(s2.at[:, cs], piece, to) for _, to in to_all], sems, size)
        piece[...] = total

    def start_ag2(n):
        c0, nc, first = CHUNKS[n]
        cs = pl.ds(c0, nc)
        sems = both(w_s, w_r, n, 3)
        ag1[n].wait_recv()
        if first == "y":
            piece, to_all, size = wf.at[ds(64 * y, 64), cs], y_peers, r1y.at[:, :, cs]
        else:
            piece, to_all, size = wf.at[ds(32 * z, 32), cs], z_peers, r1z.at[:, :, cs]
        ag2[n] = send([(piece, piece, to) for _, to in to_all], sems, size)

    for n in range(len(CHUNKS)):
        start_rs1(n)
    g1.wait_recv()
    total = gpart[ds(8 * y, 8), :]
    for i in range(NY - 1):
        total = total + gyrecv[i]
    gz[z] = total
    g2 = send([(gz.at[z], gz.at[z], to) for _, to in z_peers], both(g_s, g_r, 1), gz.at[pl.ds(0, NZ - 1)])
    start_rs2(1)
    start_rs2(2)
    start_rs2(3)
    start_rs2(0)
    g2.wait_recv()
    total = gz[0]
    for i in range(1, NZ):
        total = total + gz[i]
    mine = gsum.at[x, c, ds(8 * y, 8)]
    mine[...] = total
    g3 = send(
        [(mine, mine, dev(z, peer_y(j), peer_x(i), c)) for i in range(NX) for j in range(NY) if i or j],
        both(g_s, g_r, 2), w.at[pl.ds(0, 8 * (NX * NY - 1)), pl.ds(0, RANK)],
    )
    start_ag1(1)
    start_rs2(4)
    start_ag1(2)
    start_ag1(0)
    g3.wait_recv()
    ours = gsum.at[:, c]
    g4 = send([(ours, ours, other)], both(g_s, g_r, 3), ours)
    start_ag1(3)
    start_ag2(1)
    g4.wait_recv()
    for i in range(NX):
        for k in range(2):
            gmat[64 * i + 32 * k : 64 * i + 32 * k + 32, :] = gsum[i, k]

    plan = {
        0: [(start_ag1, 4), (start_ag2, 0)],
        2: [(start_ag2, 2)],
        4: [(start_ag2, 3)],
        7: [(start_ag2, 4)],
    }
    panels = []

    def service():
        for step, n in plan.get(len(panels), ()):
            step(n)
        panels.append(0)

    cholesky_inverse(gmat, service)
    row = lax.broadcasted_iota(jnp.int32, (RANK, RANK), 0)
    lane = lax.broadcasted_iota(jnp.int32, (RANK, RANK), 1)
    inv = split(jnp.where(row >= lane, gmat[...], 0.0))
    q = dot3(split(pfull[0]), (inv[0][:, :HALF], inv[1][:, :HALF]), 1, 1)
    q = q + dot3(split(pfull[1]), (inv[0][:, HALF:], inv[1][:, HALF:]), 1, 1)
    parts, squares = {}, 0.0
    for ns in ((0, 1, 2), (3,), (4,)):
        for n in ns:
            ag2[n].wait_recv()
        c0, c1 = CHUNKS[ns[0]][0], CHUNKS[ns[-1]][0] + CHUNKS[ns[-1]][1]
        parts[c0] = dot3(inv, split(wf[:, c0:c1]), 1, 0)
        for k in range(0, c1 - c0, 128):
            piece = parts[c0][:, k : k + 128]
            squares = squares + piece * piece
    rt = jnp.concatenate([parts[c0] for c0 in sorted(parts)], axis=1)
    squares = squares.T
    total = squares[0:8, :]
    for k in range(1, 16):
        total = total + squares[8 * k : 8 * k + 8, :]
    nbuf[ti] = total
    n1 = send([(nbuf.at[ti], nbuf.at[ti], p) for p in tensor_peers], both(n_s, n_r, 0), nbuf.at[pl.ds(0, 2 * NX - 1)])
    rsplit = split(rt)
    rh_ref[...], rl_ref[...] = rsplit
    for k in range(2):
        rows = ds(256 * (1 - c if k == 0 else c), 256)
        qk = jnp.where(c == k, q[256:], q[:256])
        nm_ref[rows, :] = mv[k] + gv[k].astype(F32) - dot3(split(0.5 * qk), rsplit, 1, 0)
    rtt_ref[...] = rt.T
    n1.wait_recv()
    total = nbuf[0]
    for i in range(1, 2 * NX):
        total = total + nbuf[i]
    total = jnp.sum(total, axis=0, keepdims=True)
    scale = lax.rsqrt(total / COLS + 1e-06)
    norm_ref[...] = jnp.broadcast_to(scale, (8, RANK))
    q_ref[...] = q * (scale * (0.2 * math.sqrt(ROWS / RANK)))
    load_w.wait()
    for cp in pending:
        cp.wait_send()


def output_kernel(nm_ref, wv_ref, q_ref, rh_ref, rl_ref, rtt_ref, norm_ref, onm_ref, onw_ref, onr_ref, nw, nr, sems):
    copies = [pltpu.make_async_copy(nm_ref, onm_ref, sems.at[0])]
    copies[0].start()
    nr[...] = rtt_ref[...] * norm_ref[0:1, :]
    copies.append(pltpu.make_async_copy(nr, onr_ref, sems.at[1]))
    copies[1].start()
    right = (rh_ref[...], rl_ref[...])
    for k in range(2):
        rows = pl.ds(256 * k, 256)
        nw[rows, :] = wv_ref[rows, :] - dot3(split(q_ref[rows, :]), right, 1, 0)
        copies.append(pltpu.make_async_copy(nw.at[rows], onw_ref.at[rows], sems.at[2 + k]))
        copies[2 + k].start()
    for cp in copies:
        cp.wait()


def hbm(array):
    return pltpu.with_memory_space_constraint(array, pltpu.HBM)


def body(momentum, gradient, weights, prior_right):
    vmem = pl.BlockSpec(memory_space=pltpu.VMEM)
    dma = pltpu.SemaphoreType.DMA
    inner = (
        pltpu.VMEM((BR, BC), F32),
        pltpu.VMEM((BR, BC), F32),
        pltpu.VMEM((BR, RANK), F32),
        pltpu.VMEM((RANK, BC), BF16),
        pltpu.VMEM((RANK, BC), BF16),
        pltpu.VMEM((BC, RANK), F32),
        pltpu.VMEM((8, RANK), F32),
    )
    factors = pl.pallas_call(
        factor_kernel,
        out_shape=inner,
        in_specs=[pl.BlockSpec(memory_space=pltpu.HBM)] * 4,
        out_specs=(vmem,) * len(inner),
        scratch_shapes=[
            pltpu.VMEM((2, 256, BC), F32),
            pltpu.VMEM((2, 256, BC), BF16),
            pltpu.VMEM((BC, RANK), F32),
            pltpu.VMEM((BR, BC), BF16),
            pltpu.VMEM((BR, BC), BF16),
            pltpu.VMEM((2, 256, HALF), F32),
            pltpu.VMEM((2, 256, HALF), F32),
            pltpu.VMEM((2, 256, HALF), F32),
            pltpu.VMEM((2, NX - 1, 64, HALF), F32),
            pltpu.VMEM((2, 64, HALF), F32),
            pltpu.VMEM((2, BR, HALF), F32),
            pltpu.VMEM((RANK, BR), F32),
            pltpu.VMEM((32, RANK), F32),
            pltpu.VMEM((NY - 1, 8, RANK), F32),
            pltpu.VMEM((NZ, 8, RANK), F32),
            pltpu.VMEM((NX, 2, 32, RANK), F32),
            pltpu.VMEM((RANK, RANK), F32),
            pltpu.VMEM((RANK, BC), F32),
            pltpu.VMEM((RANK, BC), F32),
            pltpu.VMEM((NY - 1, 64, BC), F32),
            pltpu.VMEM((NZ - 1, 32, BC), F32),
            pltpu.VMEM((64, BC), F32),
            pltpu.VMEM((32, BC), F32),
            pltpu.VMEM((NY - 1, 8, BC), F32),
            pltpu.VMEM((NZ - 1, 8, BC), F32),
            pltpu.VMEM((8, BC), F32),
            pltpu.VMEM((2 * NX, 8, RANK), F32),
            dma((6,)),
            dma((2, 2)), dma((2, 2)),
            dma((2, 2)), dma((2, 2)),
            dma((4,)), dma((4,)),
            dma((len(CHUNKS), 4)), dma((len(CHUNKS), 4)),
            dma((1,)), dma((1,)),
        ],
        compiler_params=pltpu.CompilerParams(
            collective_id=0, has_side_effects=True, vmem_limit_bytes=40 * 1024 * 1024
        ),
        name="factors",
    )(hbm(momentum), hbm(gradient), hbm(weights), hbm(prior_right))
    return pl.pallas_call(
        output_kernel,
        out_shape=(
            jax.ShapeDtypeStruct((BR, BC), F32),
            jax.ShapeDtypeStruct((BR, BC), F32),
            jax.ShapeDtypeStruct((BC, RANK), F32),
        ),
        in_specs=[vmem] * len(inner),
        out_specs=(pl.BlockSpec(memory_space=pltpu.HBM),) * 3,
        scratch_shapes=[pltpu.VMEM((BR, BC), F32), pltpu.VMEM((BC, RANK), F32), dma((4,))],
        compiler_params=pltpu.CompilerParams(vmem_limit_bytes=40 * 1024 * 1024),
        name="outputs",
    )(*[pltpu.with_memory_space_constraint(a, pltpu.VMEM) for a in factors])


def solution(mesh):
    in_specs = (P("fsdp", "tensor"), P("fsdp", "tensor"), P("fsdp", "tensor"), P("tensor", None))
    out_specs = (P("fsdp", "tensor"), P("fsdp", "tensor"), P("tensor", None))
    return jax.shard_map(body, mesh=mesh, in_specs=in_specs, out_specs=out_specs, check_vma=False)
```

```python
import functools
import math

import jax
import jax.numpy as jnp
from jax import lax
from jax.experimental import pallas as pl
from jax.experimental.pallas import tpu as pltpu
from jax.sharding import PartitionSpec as P

ROWS = 16384
COLS = 9216
RANK = 256
NZ, NY, NX = 8, 4, 4
BR = 512
BC = 1152
HALF = 128
LEAF = 64
PANEL = 16
F32 = jnp.float32
BF16 = jnp.bfloat16
MESH = pl.DeviceIdType.MESH
CHUNKS = ((0, 256, "z"), (256, 256, "y"), (512, 256, "y"), (768, 256, "y"), (1024, 128, "y"))


def dot_f32(a, b, ca, cb):
    return lax.dot_general(
        a, b, (((ca,), (cb,)), ((), ())), precision=lax.Precision.HIGHEST, preferred_element_type=F32
    )


def split(a):
    hi = a.astype(BF16)
    return hi, (a - hi.astype(F32)).astype(BF16)


def dot_bf16(a, b, ca, cb):
    return lax.dot_general(a, b, (((ca,), (cb,)), ((), ())), preferred_element_type=F32)


def dot3(a, b, ca, cb):
    return dot_bf16(
        jnp.concatenate([a[0], a[0], a[1]], axis=ca), jnp.concatenate([b[1], b[0], b[0]], axis=cb), ca, cb
    )


def leaf_elimination(block, service):
    n = block.shape[0]
    row = lax.broadcasted_iota(jnp.int32, (n, n), 0)
    lane = lax.broadcasted_iota(jnp.int32, (n, n), 1)
    for p0 in range(0, n, PANEL):
        cols = [jnp.broadcast_to(block[p0:, p0 + j : p0 + j + 1], (n - p0, n)) for j in range(PANEL)]
        rw, ln, low = row[p0:], lane[p0:], block[p0:]
        for k in range(PANEL):
            r = 1.0 / cols[k][k : k + 1, :]
            below = jnp.where(rw > p0 + k, cols[k], 0.0)
            for j in range(k + 1, PANEL):
                cols[j] = cols[j] - below * (cols[j][k : k + 1, :] * r)
            pivot_row = jnp.where(ln[0:1] == p0 + k, 1.0, low[k : k + 1, :]) * r
            cleared = jnp.where((ln == p0 + k) & (rw > p0 + k), 0.0, low)
            low = cleared - below * pivot_row
        block = jnp.concatenate([block[:p0], low], axis=0) if p0 else low
        service()
    return block


def cholesky_inverse(a, service):
    blocks = RANK // LEAF
    for j in range(blocks):
        s = slice(j * LEAF, (j + 1) * LEAF)
        d = leaf_elimination(a[s, s], service)
        row = lax.broadcasted_iota(jnp.int32, (LEAF, LEAF), 0)
        lane = lax.broadcasted_iota(jnp.int32, (LEAF, LEAF), 1)
        pivot = jnp.sum(jnp.where(row == lane, d, 0.0), axis=1, keepdims=True)
        unit = jnp.where(row > lane, d, jnp.where(row == lane, 1.0, 0.0))
        inv = unit * lax.rsqrt(pivot)
        x = dot_f32(inv, a[s, :], 1, 0)
        a[s, :] = x
        a[s, s] = inv
        if j < blocks - 1:
            low = (j + 1) * LEAF
            a[low:, s] = jnp.zeros((RANK - low, LEAF), F32)
            a[low:, :] = a[low:, :] - dot_f32(x[:, low:], a[s, :], 0, 0)


def factor_kernel(
    m_ref, g_ref, wt_ref, v_ref, nm_ref, wv_ref, q_ref, rh_ref, rl_ref, rtt_ref, norm_ref,
    mv, gv, vv, bh, bl, part, crecv, half, xrecv, own, pfull, pt,
    gpart, gyrecv, gz, gsum, gmat,
    w, wf, r1y, r1z, s1y, s1z, r2y, r2z, s2,
    nbuf, l_s, c_s, c_r, x_s, x_r, g_s, g_r, w_s, w_r, n_s, n_r,
):
    fi, ti = lax.axis_index("fsdp"), lax.axis_index("tensor")
    z, y = fi // NY, lax.rem(fi, NY)
    x, c = ti // 2, lax.rem(ti, 2)

    def dev(zz, yy, xx, cc):
        return (zz * NY + yy, xx * 2 + cc)

    def peer_z(i):
        return lax.rem(z + i, NZ)

    def peer_y(i):
        return lax.rem(y + i, NY)

    def peer_x(i):
        return lax.rem(x + i, NX)

    def ds(start, size):
        return pl.ds(pl.multiple_of(start, size if size < 16 else 16), size)

    pending = []

    def send(copies, sems, size):
        for src, dst, to in copies:
            pltpu.make_async_remote_copy(
                src_ref=src, dst_ref=dst, send_sem=sems[0], recv_sem=sems[1], device_id=to, device_id_type=MESH
            ).start()
        group = pltpu.make_async_remote_copy(
            src_ref=size, dst_ref=size, send_sem=sems[0], recv_sem=sems[1], device_id=copies[0][2], device_id_type=MESH
        )
        pending.append(group)
        return group

    def both(sem_s, sem_r, *at):
        return sem_s.at[at], sem_r.at[at]

    load_v = pltpu.make_async_copy(v_ref, vv, l_s.at[0])
    load_v.start()
    loads = []
    for k, cc in enumerate((1 - c, c)):
        rows = ds(256 * cc, 256)
        loads.append([
            pltpu.make_async_copy(m_ref.at[rows], mv.at[k], l_s.at[1 + 2 * k]),
            pltpu.make_async_copy(g_ref.at[rows], gv.at[k], l_s.at[2 + 2 * k]),
        ])
        for cp in loads[k]:
            cp.start()

    barrier = pltpu.get_barrier_semaphore()
    peers = [dev(z, peer_y(i), x, c) for i in range(1, NY)]
    peers += [dev(peer_z(i), y, x, c) for i in range(1, NZ)]
    tensor_peers = [dev(z, y, x, 1 - c)]
    tensor_peers += [dev(z, y, peer_x(i), cc) for i in range(1, NX) for cc in (c, 1 - c)]
    plane_peers = [dev(z, peer_y(j), peer_x(i), c) for i in range(1, NX) for j in range(1, NY)]
    everyone = peers + tensor_peers + plane_peers
    for p in everyone:
        pl.semaphore_signal(barrier, inc=1, device_id=p, device_id_type=MESH)

    load_v.wait()
    vs = split(vv[...])

    def projected(k, cc):
        for cp in loads[k]:
            cp.wait()
        rows = ds(256 * cc, 256)
        hi, lo = split(mv[k] + gv[k].astype(F32))
        bh[rows, :] = hi
        bl[rows, :] = lo
        return dot3((hi, lo), vs, 1, 0)

    other = dev(z, y, x, 1 - c)
    x_peers = [(i, dev(z, y, peer_x(i), c)) for i in range(1, NX)]
    core_rs, x_rs, x_ag = [], [], []
    theirs = projected(0, 1 - c)
    for h in range(2):
        part[h] = theirs[:, h * HALF : (h + 1) * HALF]
    pl.semaphore_wait(barrier, len(everyone))
    for h in range(2):
        core_rs.append(send([(part.at[h], crecv.at[h], other)], both(c_s, c_r, h, 0), crecv.at[h]))
    ours = projected(1, c)
    load_w = pltpu.make_async_copy(wt_ref, wv_ref, l_s.at[5])
    load_w.start()
    for h in range(2):
        core_rs[h].wait_recv()
        half[h] = ours[:, h * HALF : (h + 1) * HALF] + crecv[h]
        x_rs.append(send(
            [(half.at[h, ds(64 * peer_x(i), 64)], xrecv.at[h, i - 1], to) for i, to in x_peers],
            both(x_s, x_r, h, 0), xrecv.at[h],
        ))
    for h in range(2):
        x_rs[h].wait_recv()
        total = half[h, ds(64 * x, 64), :]
        for i in range(NX - 1):
            total = total + xrecv[h, i]
        own[h] = total
        piece = pfull.at[h, ds(256 * c + 64 * x, 64)]
        x_ag.append(send([(own.at[h], piece, to) for _, to in x_peers], both(x_s, x_r, h, 1), xrecv.at[h]))
        pfull[h, ds(256 * c + 64 * x, 64), :] = total
    for h in range(2):
        x_ag[h].wait_recv()
        piece = pfull.at[h, ds(256 * c, 256)]
        send([(piece, piece, other)], both(c_s, c_r, h, 1), piece).wait_recv()
        ph = pfull[h].T
        pt[h * HALF : (h + 1) * HALF, :] = ph
        if h == 0:
            w[:HALF, :] = dot3(split(ph), (bh[...], bl[...]), 1, 0)

    rows = ds(32 * ti, 32)
    ptr = pt[rows, :]
    for h in range(2):
        gpart[:, h * HALF : (h + 1) * HALF] = dot_f32(ptr, pfull[h], 1, 0)
    g1 = send(
        [(gpart.at[ds(8 * peer_y(i), 8)], gyrecv.at[i - 1], dev(z, peer_y(i), x, c)) for i in range(1, NY)],
        both(g_s, g_r, 0), gyrecv,
    )
    w[HALF:, :] = dot3(split(ph), (bh[...], bl[...]), 1, 0)

    y_peers = [(i, dev(z, peer_y(i), x, c)) for i in range(1, NY)]
    z_peers = [(i, dev(peer_z(i), y, x, c)) for i in range(1, NZ)]
    rs1, rs2, ag1, ag2 = {}, {}, {}, {}

    def start_rs1(n):
        c0, nc, first = CHUNKS[n]
        cs = pl.ds(c0, nc)
        sems = both(w_s, w_r, n, 0)
        if first == "y":
            rs1[n] = send(
                [(w.at[ds(64 * peer_y(i), 64), cs], r1y.at[i - 1, :, cs], to) for i, to in y_peers], sems, r1y.at[:, :, cs]
            )
        else:
            rs1[n] = send(
                [(w.at[ds(32 * peer_z(i), 32), cs], r1z.at[i - 1, :, cs], to) for i, to in z_peers], sems, r1z.at[:, :, cs]
            )

    def start_rs2(n):
        c0, nc, first = CHUNKS[n]
        cs = pl.ds(c0, nc)
        sems = both(w_s, w_r, n, 1)
        rs1[n].wait_recv()
        if first == "y":
            total = w[ds(64 * y, 64), cs]
            for i in range(NY - 1):
                total = total + r1y[i, :, cs]
            s1y[:, cs] = total
            rs2[n] = send(
                [(s1y.at[ds(8 * peer_z(i), 8), cs], r2z.at[i - 1, :, cs], to) for i, to in z_peers], sems, r2z.at[:, :, cs]
            )
        else:
            total = w[ds(32 * z, 32), cs]
            for i in range(NZ - 1):
                total = total + r1z[i, :, cs]
            s1z[:, cs] = total
            rs2[n] = send(
                [(s1z.at[ds(8 * peer_y(i), 8), cs], r2y.at[i - 1, :, cs], to) for i, to in y_peers], sems, r2y.at[:, :, cs]
            )

    def start_ag1(n):
        c0, nc, first = CHUNKS[n]
        cs = pl.ds(c0, nc)
        sems = both(w_s, w_r, n, 2)
        rs2[n].wait_recv()
        if first == "y":
            total = s1y[ds(8 * z, 8), cs]
            for i in range(NZ - 1):
                total = total + r2z[i, :, cs]
            piece, to_all, size = wf.at[ds(64 * y + 8 * z, 8), cs], z_peers, r2z.at[:, :, cs]
        else:
            total = s1z[ds(8 * y, 8), cs]
            for i in range(NY - 1):
                total = total + r2y[i, :, cs]
            piece, to_all, size = wf.at[ds(32 * z + 8 * y, 8), cs], y_peers, r2y.at[:, :, cs]
        s2[:, cs] = total
        ag1[n] = send([(s2.at[:, cs], piece, to) for _, to in to_all], sems, size)
        piece[...] = total

    def start_ag2(n):
        c0, nc, first = CHUNKS[n]
        cs = pl.ds(c0, nc)
        sems = both(w_s, w_r, n, 3)
        ag1[n].wait_recv()
        if first == "y":
            piece, to_all, size = wf.at[ds(64 * y, 64), cs], y_peers, r1y.at[:, :, cs]
        else:
            piece, to_all, size = wf.at[ds(32 * z, 32), cs], z_peers, r1z.at[:, :, cs]
        ag2[n] = send([(piece, piece, to) for _, to in to_all], sems, size)

    for n in range(len(CHUNKS)):
        start_rs1(n)
    g1.wait_recv()
    total = gpart[ds(8 * y, 8), :]
    for i in range(NY - 1):
        total = total + gyrecv[i]
    gz[z] = total
    g2 = send([(gz.at[z], gz.at[z], to) for _, to in z_peers], both(g_s, g_r, 1), gz.at[pl.ds(0, NZ - 1)])
    start_rs2(1)
    start_rs2(2)
    start_rs2(3)
    start_rs2(0)
    g2.wait_recv()
    total = gz[0]
    for i in range(1, NZ):
        total = total + gz[i]
    mine = gsum.at[x, c, ds(8 * y, 8)]
    mine[...] = total
    g3 = send(
        [(mine, mine, dev(z, peer_y(j), peer_x(i), c)) for i in range(NX) for j in range(NY) if i or j],
        both(g_s, g_r, 2), w.at[pl.ds(0, 8 * (NX * NY - 1)), pl.ds(0, RANK)],
    )
    start_ag1(1)
    start_rs2(4)
    start_ag1(2)
    start_ag1(0)
    g3.wait_recv()
    ours = gsum.at[:, c]
    g4 = send([(ours, ours, other)], both(g_s, g_r, 3), ours)
    start_ag1(3)
    start_ag2(1)
    g4.wait_recv()
    for i in range(NX):
        for k in range(2):
            gmat[64 * i + 32 * k : 64 * i + 32 * k + 32, :] = gsum[i, k]

    plan = {
        0: [(start_ag1, 4), (start_ag2, 0)],
        2: [(start_ag2, 2)],
        4: [(start_ag2, 3)],
        7: [(start_ag2, 4)],
    }
    panels = []

    def service():
        for step, n in plan.get(len(panels), ()):
            step(n)
        panels.append(0)

    cholesky_inverse(gmat, service)
    row = lax.broadcasted_iota(jnp.int32, (RANK, RANK), 0)
    lane = lax.broadcasted_iota(jnp.int32, (RANK, RANK), 1)
    inv = split(jnp.where(row >= lane, gmat[...], 0.0))
    parts, squares = {}, 0.0
    for ns in ((0, 1, 2), (3,), (4,)):
        for n in ns:
            ag2[n].wait_recv()
        c0, c1 = CHUNKS[ns[0]][0], CHUNKS[ns[-1]][0] + CHUNKS[ns[-1]][1]
        parts[c0] = dot3(inv, split(wf[:, c0:c1]), 1, 0)
        for k in range(0, c1 - c0, 128):
            piece = parts[c0][:, k : k + 128]
            squares = squares + piece * piece
    rt = jnp.concatenate([parts[c0] for c0 in sorted(parts)], axis=1)
    squares = squares.T
    total = squares[0:8, :]
    for k in range(1, 16):
        total = total + squares[8 * k : 8 * k + 8, :]
    nbuf[ti] = total
    n1 = send([(nbuf.at[ti], nbuf.at[ti], p) for p in tensor_peers], both(n_s, n_r, 0), nbuf.at[pl.ds(0, 2 * NX - 1)])
    q = dot3(split(pfull[0]), (inv[0][:, :HALF], inv[1][:, :HALF]), 1, 1)
    q = q + dot3(split(pfull[1]), (inv[0][:, HALF:], inv[1][:, HALF:]), 1, 1)
    rsplit = split(rt)
    rh_ref[...], rl_ref[...] = rsplit
    for k in range(2):
        rows = ds(256 * (1 - c if k == 0 else c), 256)
        qk = jnp.where(c == k, q[256:], q[:256])
        nm_ref[rows, :] = mv[k] + gv[k].astype(F32) - dot3(split(0.5 * qk), rsplit, 1, 0)
    rtt_ref[...] = rt.T
    load_w.wait()
    for cp in pending[:-1]:
        cp.wait_send()
    n1.wait_recv()
    total = nbuf[0]
    for i in range(1, 2 * NX):
        total = total + nbuf[i]
    total = jnp.sum(total, axis=0, keepdims=True)
    scale = lax.rsqrt(total / COLS + 1e-06)
    norm_ref[...] = jnp.broadcast_to(scale, (8, RANK))
    q_ref[...] = q * (scale * (0.2 * math.sqrt(ROWS / RANK)))
    n1.wait_send()


def output_kernel(nm_ref, wv_ref, q_ref, rh_ref, rl_ref, rtt_ref, norm_ref, onm_ref, onw_ref, onr_ref, nw, nr, sems):
    copies = [pltpu.make_async_copy(nm_ref, onm_ref, sems.at[0])]
    copies[0].start()
    nr[...] = rtt_ref[...] * norm_ref[0:1, :]
    copies.append(pltpu.make_async_copy(nr, onr_ref, sems.at[1]))
    copies[1].start()
    right = (rh_ref[...], rl_ref[...])
    for k in range(2):
        rows = pl.ds(256 * k, 256)
        nw[rows, :] = wv_ref[rows, :] - dot3(split(q_ref[rows, :]), right, 1, 0)
        copies.append(pltpu.make_async_copy(nw.at[rows], onw_ref.at[rows], sems.at[2 + k]))
        copies[2 + k].start()
    for cp in copies:
        cp.wait()


def hbm(array):
    return pltpu.with_memory_space_constraint(array, pltpu.HBM)


def body(momentum, gradient, weights, prior_right):
    vmem = pl.BlockSpec(memory_space=pltpu.VMEM)
    dma = pltpu.SemaphoreType.DMA
    inner = (
        pltpu.VMEM((BR, BC), F32),
        pltpu.VMEM((BR, BC), F32),
        pltpu.VMEM((BR, RANK), F32),
        pltpu.VMEM((RANK, BC), BF16),
        pltpu.VMEM((RANK, BC), BF16),
        pltpu.VMEM((BC, RANK), F32),
        pltpu.VMEM((8, RANK), F32),
    )
    factors = pl.pallas_call(
        factor_kernel,
        out_shape=inner,
        in_specs=[pl.BlockSpec(memory_space=pltpu.HBM)] * 4,
        out_specs=(vmem,) * len(inner),
        scratch_shapes=[
            pltpu.VMEM((2, 256, BC), F32),
            pltpu.VMEM((2, 256, BC), BF16),
            pltpu.VMEM((BC, RANK), F32),
            pltpu.VMEM((BR, BC), BF16),
            pltpu.VMEM((BR, BC), BF16),
            pltpu.VMEM((2, 256, HALF), F32),
            pltpu.VMEM((2, 256, HALF), F32),
            pltpu.VMEM((2, 256, HALF), F32),
            pltpu.VMEM((2, NX - 1, 64, HALF), F32),
            pltpu.VMEM((2, 64, HALF), F32),
            pltpu.VMEM((2, BR, HALF), F32),
            pltpu.VMEM((RANK, BR), F32),
            pltpu.VMEM((32, RANK), F32),
            pltpu.VMEM((NY - 1, 8, RANK), F32),
            pltpu.VMEM((NZ, 8, RANK), F32),
            pltpu.VMEM((NX, 2, 32, RANK), F32),
            pltpu.VMEM((RANK, RANK), F32),
            pltpu.VMEM((RANK, BC), F32),
            pltpu.VMEM((RANK, BC), F32),
            pltpu.VMEM((NY - 1, 64, BC), F32),
            pltpu.VMEM((NZ - 1, 32, BC), F32),
            pltpu.VMEM((64, BC), F32),
            pltpu.VMEM((32, BC), F32),
            pltpu.VMEM((NY - 1, 8, BC), F32),
            pltpu.VMEM((NZ - 1, 8, BC), F32),
            pltpu.VMEM((8, BC), F32),
            pltpu.VMEM((2 * NX, 8, RANK), F32),
            dma((6,)),
            dma((2, 2)), dma((2, 2)),
            dma((2, 2)), dma((2, 2)),
            dma((4,)), dma((4,)),
            dma((len(CHUNKS), 4)), dma((len(CHUNKS), 4)),
            dma((1,)), dma((1,)),
        ],
        compiler_params=pltpu.CompilerParams(
            collective_id=0, has_side_effects=True, vmem_limit_bytes=40 * 1024 * 1024
        ),
        name="factors",
    )(hbm(momentum), hbm(gradient), hbm(weights), hbm(prior_right))
    return pl.pallas_call(
        output_kernel,
        out_shape=(
            jax.ShapeDtypeStruct((BR, BC), F32),
            jax.ShapeDtypeStruct((BR, BC), F32),
            jax.ShapeDtypeStruct((BC, RANK), F32),
        ),
        in_specs=[vmem] * len(inner),
        out_specs=(pl.BlockSpec(memory_space=pltpu.HBM),) * 3,
        scratch_shapes=[pltpu.VMEM((BR, BC), F32), pltpu.VMEM((BC, RANK), F32), dma((4,))],
        compiler_params=pltpu.CompilerParams(vmem_limit_bytes=40 * 1024 * 1024),
        name="outputs",
    )(*[pltpu.with_memory_space_constraint(a, pltpu.VMEM) for a in factors])


def solution(mesh):
    in_specs = (P("fsdp", "tensor"), P("fsdp", "tensor"), P("fsdp", "tensor"), P("tensor", None))
    out_specs = (P("fsdp", "tensor"), P("fsdp", "tensor"), P("tensor", None))
    return jax.shard_map(body, mesh=mesh, in_specs=in_specs, out_specs=out_specs, check_vma=False)
```

```python
import functools
import math

import jax
import jax.numpy as jnp
from jax import lax
from jax.experimental import pallas as pl
from jax.experimental.pallas import tpu as pltpu
from jax.sharding import PartitionSpec as P

ROWS = 16384
COLS = 9216
RANK = 256
NZ, NY, NX = 8, 4, 4
BR = 512
BC = 1152
HALF = 128
LEAF = 64
PANEL = 16
F32 = jnp.float32
BF16 = jnp.bfloat16
MESH = pl.DeviceIdType.MESH
CHUNKS = ((0, 256, "z"), (256, 256, "y"), (512, 256, "y"), (768, 256, "y"), (1024, 128, "y"))


def dot_f32(a, b, ca, cb):
    return lax.dot_general(
        a, b, (((ca,), (cb,)), ((), ())), precision=lax.Precision.HIGHEST, preferred_element_type=F32
    )


def split(a):
    hi = a.astype(BF16)
    return hi, (a - hi.astype(F32)).astype(BF16)


def dot_bf16(a, b, ca, cb):
    return lax.dot_general(a, b, (((ca,), (cb,)), ((), ())), preferred_element_type=F32)


def dot3(a, b, ca, cb):
    return dot_bf16(
        jnp.concatenate([a[0], a[0], a[1]], axis=ca), jnp.concatenate([b[1], b[0], b[0]], axis=cb), ca, cb
    )


def leaf_elimination(block, service):
    n = block.shape[0]
    row = lax.broadcasted_iota(jnp.int32, (n, n), 0)
    lane = lax.broadcasted_iota(jnp.int32, (n, n), 1)
    for p0 in range(0, n, PANEL):
        cols = [jnp.broadcast_to(block[p0:, p0 + j : p0 + j + 1], (n - p0, n)) for j in range(PANEL)]
        rw, ln, low = row[p0:], lane[p0:], block[p0:]
        for k in range(PANEL):
            r = 1.0 / cols[k][k : k + 1, :]
            below = jnp.where(rw > p0 + k, cols[k], 0.0)
            for j in range(k + 1, PANEL):
                cols[j] = cols[j] - below * (cols[j][k : k + 1, :] * r)
            pivot_row = jnp.where(ln[0:1] == p0 + k, 1.0, low[k : k + 1, :]) * r
            cleared = jnp.where((ln == p0 + k) & (rw > p0 + k), 0.0, low)
            low = cleared - below * pivot_row
        block = jnp.concatenate([block[:p0], low], axis=0) if p0 else low
        service()
    return block


def cholesky_inverse(a, service):
    blocks = RANK // LEAF
    for j in range(blocks):
        s = slice(j * LEAF, (j + 1) * LEAF)
        d = leaf_elimination(a[s, s], service)
        row = lax.broadcasted_iota(jnp.int32, (LEAF, LEAF), 0)
        lane = lax.broadcasted_iota(jnp.int32, (LEAF, LEAF), 1)
        pivot = jnp.sum(jnp.where(row == lane, d, 0.0), axis=1, keepdims=True)
        unit = jnp.where(row > lane, d, jnp.where(row == lane, 1.0, 0.0))
        inv = unit * lax.rsqrt(pivot)
        x = dot_f32(inv, a[s, :], 1, 0)
        a[s, :] = x
        a[s, s] = inv
        if j < blocks - 1:
            low = (j + 1) * LEAF
            a[low:, s] = jnp.zeros((RANK - low, LEAF), F32)
            a[low:, :] = a[low:, :] - dot_f32(x[:, low:], a[s, :], 0, 0)


def factor_kernel(
    m_ref, g_ref, wt_ref, v_ref, nm_ref, wv_ref, q_ref, rh_ref, rl_ref, rtt_ref, norm_ref,
    mv, gv, vv, bh, bl, part, crecv, half, xrecv, own, pfull, pt,
    gpart, gyrecv, gz, gsum, gmat,
    w, wf, r1y, r1z, s1y, s1z, r2y, r2z, s2,
    nbuf, l_s, c_s, c_r, x_s, x_r, g_s, g_r, w_s, w_r, n_s, n_r,
):
    fi, ti = lax.axis_index("fsdp"), lax.axis_index("tensor")
    z, y = fi // NY, lax.rem(fi, NY)
    x, c = ti // 2, lax.rem(ti, 2)

    def dev(zz, yy, xx, cc):
        return (zz * NY + yy, xx * 2 + cc)

    def peer_z(i):
        return lax.rem(z + i, NZ)

    def peer_y(i):
        return lax.rem(y + i, NY)

    def peer_x(i):
        return lax.rem(x + i, NX)

    def ds(start, size):
        return pl.ds(pl.multiple_of(start, size if size < 16 else 16), size)

    pending = []

    def send(copies, sems, size):
        for src, dst, to in copies:
            pltpu.make_async_remote_copy(
                src_ref=src, dst_ref=dst, send_sem=sems[0], recv_sem=sems[1], device_id=to, device_id_type=MESH
            ).start()
        group = pltpu.make_async_remote_copy(
            src_ref=size, dst_ref=size, send_sem=sems[0], recv_sem=sems[1], device_id=copies[0][2], device_id_type=MESH
        )
        pending.append(group)
        return group

    def both(sem_s, sem_r, *at):
        return sem_s.at[at], sem_r.at[at]

    load_v = pltpu.make_async_copy(v_ref, vv, l_s.at[0])
    load_v.start()
    loads = []
    for k, cc in enumerate((1 - c, c)):
        rows = ds(256 * cc, 256)
        loads.append([
            pltpu.make_async_copy(m_ref.at[rows], mv.at[k], l_s.at[1 + 2 * k]),
            pltpu.make_async_copy(g_ref.at[rows], gv.at[k], l_s.at[2 + 2 * k]),
        ])
        for cp in loads[k]:
            cp.start()

    barrier = pltpu.get_barrier_semaphore()
    peers = [dev(z, peer_y(i), x, c) for i in range(1, NY)]
    peers += [dev(peer_z(i), y, x, c) for i in range(1, NZ)]
    tensor_peers = [dev(z, y, x, 1 - c)]
    tensor_peers += [dev(z, y, peer_x(i), cc) for i in range(1, NX) for cc in (c, 1 - c)]
    plane_peers = [dev(z, peer_y(j), peer_x(i), c) for i in range(1, NX) for j in range(1, NY)]
    everyone = peers + tensor_peers + plane_peers
    for p in everyone:
        pl.semaphore_signal(barrier, inc=1, device_id=p, device_id_type=MESH)

    load_v.wait()
    vs = split(vv[...])

    def projected(k, cc):
        for cp in loads[k]:
            cp.wait()
        rows = ds(256 * cc, 256)
        hi, lo = split(mv[k] + gv[k].astype(F32))
        bh[rows, :] = hi
        bl[rows, :] = lo
        return dot3((hi, lo), vs, 1, 0)

    other = dev(z, y, x, 1 - c)
    x_peers = [(i, dev(z, y, peer_x(i), c)) for i in range(1, NX)]
    core_rs, x_rs, x_ag = [], [], []
    theirs = projected(0, 1 - c)
    for h in range(2):
        part[h] = theirs[:, h * HALF : (h + 1) * HALF]
    pl.semaphore_wait(barrier, len(everyone))
    for h in range(2):
        core_rs.append(send([(part.at[h], crecv.at[h], other)], both(c_s, c_r, h, 0), crecv.at[h]))
    ours = projected(1, c)
    load_w = pltpu.make_async_copy(wt_ref, wv_ref, l_s.at[5])
    load_w.start()
    for h in range(2):
        core_rs[h].wait_recv()
        half[h] = ours[:, h * HALF : (h + 1) * HALF] + crecv[h]
        x_rs.append(send(
            [(half.at[h, ds(64 * peer_x(i), 64)], xrecv.at[h, i - 1], to) for i, to in x_peers],
            both(x_s, x_r, h, 0), xrecv.at[h],
        ))
    for h in range(2):
        x_rs[h].wait_recv()
        total = half[h, ds(64 * x, 64), :]
        for i in range(NX - 1):
            total = total + xrecv[h, i]
        own[h] = total
        piece = pfull.at[h, ds(256 * c + 64 * x, 64)]
        x_ag.append(send([(own.at[h], piece, to) for _, to in x_peers], both(x_s, x_r, h, 1), xrecv.at[h]))
        pfull[h, ds(256 * c + 64 * x, 64), :] = total
    for h in range(2):
        x_ag[h].wait_recv()
        piece = pfull.at[h, ds(256 * c, 256)]
        send([(piece, piece, other)], both(c_s, c_r, h, 1), piece).wait_recv()
        ph = pfull[h].T
        pt[h * HALF : (h + 1) * HALF, :] = ph
        if h == 0:
            w[:HALF, :] = dot3(split(ph), (bh[...], bl[...]), 1, 0)

    rows = ds(64 * x, 64)
    ptr = pt[rows, :]
    for h in range(2):
        gpart[:, h * HALF : (h + 1) * HALF] = dot_f32(ptr, pfull[h], 1, 0)
    g1 = send(
        [(gpart.at[ds(16 * peer_y(i), 16)], gyrecv.at[i - 1], dev(z, peer_y(i), x, c)) for i in range(1, NY)],
        both(g_s, g_r, 0), gyrecv,
    )
    w[HALF:, :] = dot3(split(ph), (bh[...], bl[...]), 1, 0)

    y_peers = [(i, dev(z, peer_y(i), x, c)) for i in range(1, NY)]
    z_peers = [(i, dev(peer_z(i), y, x, c)) for i in range(1, NZ)]
    rs1, rs2, ag1, ag2 = {}, {}, {}, {}

    def start_rs1(n):
        c0, nc, first = CHUNKS[n]
        cs = pl.ds(c0, nc)
        sems = both(w_s, w_r, n, 0)
        if first == "y":
            rs1[n] = send(
                [(w.at[ds(64 * peer_y(i), 64), cs], r1y.at[i - 1, :, cs], to) for i, to in y_peers], sems, r1y.at[:, :, cs]
            )
        else:
            rs1[n] = send(
                [(w.at[ds(32 * peer_z(i), 32), cs], r1z.at[i - 1, :, cs], to) for i, to in z_peers], sems, r1z.at[:, :, cs]
            )

    def start_rs2(n):
        c0, nc, first = CHUNKS[n]
        cs = pl.ds(c0, nc)
        sems = both(w_s, w_r, n, 1)
        rs1[n].wait_recv()
        if first == "y":
            total = w[ds(64 * y, 64), cs]
            for i in range(NY - 1):
                total = total + r1y[i, :, cs]
            s1y[:, cs] = total
            rs2[n] = send(
                [(s1y.at[ds(8 * peer_z(i), 8), cs], r2z.at[i - 1, :, cs], to) for i, to in z_peers], sems, r2z.at[:, :, cs]
            )
        else:
            total = w[ds(32 * z, 32), cs]
            for i in range(NZ - 1):
                total = total + r1z[i, :, cs]
            s1z[:, cs] = total
            rs2[n] = send(
                [(s1z.at[ds(8 * peer_y(i), 8), cs], r2y.at[i - 1, :, cs], to) for i, to in y_peers], sems, r2y.at[:, :, cs]
            )

    def start_ag1(n):
        c0, nc, first = CHUNKS[n]
        cs = pl.ds(c0, nc)
        sems = both(w_s, w_r, n, 2)
        rs2[n].wait_recv()
        if first == "y":
            total = s1y[ds(8 * z, 8), cs]
            for i in range(NZ - 1):
                total = total + r2z[i, :, cs]
            piece, to_all, size = wf.at[ds(64 * y + 8 * z, 8), cs], z_peers, r2z.at[:, :, cs]
        else:
            total = s1z[ds(8 * y, 8), cs]
            for i in range(NY - 1):
                total = total + r2y[i, :, cs]
            piece, to_all, size = wf.at[ds(32 * z + 8 * y, 8), cs], y_peers, r2y.at[:, :, cs]
        s2[:, cs] = total
        ag1[n] = send([(s2.at[:, cs], piece, to) for _, to in to_all], sems, size)
        piece[...] = total

    def start_ag2(n):
        c0, nc, first = CHUNKS[n]
        cs = pl.ds(c0, nc)
        sems = both(w_s, w_r, n, 3)
        ag1[n].wait_recv()
        if first == "y":
            piece, to_all, size = wf.at[ds(64 * y, 64), cs], y_peers, r1y.at[:, :, cs]
        else:
            piece, to_all, size = wf.at[ds(32 * z, 32), cs], z_peers, r1z.at[:, :, cs]
        ag2[n] = send([(piece, piece, to) for _, to in to_all], sems, size)

    for n in range(len(CHUNKS)):
        start_rs1(n)
    g1.wait_recv()
    total = gpart[ds(16 * y, 16), :]
    for i in range(NY - 1):
        total = total + gyrecv[i]
    gz[z] = total
    g2 = send([(gz.at[z], gz.at[z], to) for _, to in z_peers], both(g_s, g_r, 1), gz.at[pl.ds(0, NZ - 1)])
    start_rs2(1)
    start_rs2(2)
    start_rs2(3)
    start_rs2(0)
    g2.wait_recv()
    total = gz[0]
    for i in range(1, NZ):
        total = total + gz[i]
    mine = gsum.at[x, ds(16 * y, 16)]
    mine[...] = total
    g3 = send(
        [(mine, mine, dev(z, peer_y(j), peer_x(i), c)) for i in range(NX) for j in range(NY) if i or j],
        both(g_s, g_r, 2), w.at[pl.ds(0, 16 * (NX * NY - 1)), pl.ds(0, RANK)],
    )
    start_ag1(1)
    start_rs2(4)
    start_ag1(2)
    start_ag1(0)
    g3.wait_recv()
    start_ag1(3)
    start_ag2(1)
    for i in range(NX):
        gmat[64 * i : 64 * i + 64, :] = gsum[i]

    plan = {
        0: [(start_ag1, 4), (start_ag2, 0)],
        2: [(start_ag2, 2)],
        4: [(start_ag2, 3)],
        7: [(start_ag2, 4)],
    }
    panels = []

    def service():
        for step, n in plan.get(len(panels), ()):
            step(n)
        panels.append(0)

    cholesky_inverse(gmat, service)
    row = lax.broadcasted_iota(jnp.int32, (RANK, RANK), 0)
    lane = lax.broadcasted_iota(jnp.int32, (RANK, RANK), 1)
    inv = split(jnp.where(row >= lane, gmat[...], 0.0))
    parts, squares = {}, 0.0
    for ns in ((0, 1, 2), (3,), (4,)):
        for n in ns:
            ag2[n].wait_recv()
        c0, c1 = CHUNKS[ns[0]][0], CHUNKS[ns[-1]][0] + CHUNKS[ns[-1]][1]
        parts[c0] = dot3(inv, split(wf[:, c0:c1]), 1, 0)
        for k in range(0, c1 - c0, 128):
            piece = parts[c0][:, k : k + 128]
            squares = squares + piece * piece
    rt = jnp.concatenate([parts[c0] for c0 in sorted(parts)], axis=1)
    squares = squares.T
    total = squares[0:8, :]
    for k in range(1, 16):
        total = total + squares[8 * k : 8 * k + 8, :]
    nbuf[ti] = total
    n1 = send([(nbuf.at[ti], nbuf.at[ti], p) for p in tensor_peers], both(n_s, n_r, 0), nbuf.at[pl.ds(0, 2 * NX - 1)])
    q = dot3(split(pfull[0]), (inv[0][:, :HALF], inv[1][:, :HALF]), 1, 1)
    q = q + dot3(split(pfull[1]), (inv[0][:, HALF:], inv[1][:, HALF:]), 1, 1)
    rsplit = split(rt)
    rh_ref[...], rl_ref[...] = rsplit
    for k in range(2):
        rows = ds(256 * (1 - c if k == 0 else c), 256)
        qk = jnp.where(c == k, q[256:], q[:256])
        nm_ref[rows, :] = mv[k] + gv[k].astype(F32) - dot3(split(0.5 * qk), rsplit, 1, 0)
    rtt_ref[...] = rt.T
    load_w.wait()
    for cp in pending[:-1]:
        cp.wait_send()
    n1.wait_recv()
    total = nbuf[0]
    for i in range(1, 2 * NX):
        total = total + nbuf[i]
    total = jnp.sum(total, axis=0, keepdims=True)
    scale = lax.rsqrt(total / COLS + 1e-06)
    norm_ref[...] = jnp.broadcast_to(scale, (8, RANK))
    q_ref[...] = q * (scale * (0.2 * math.sqrt(ROWS / RANK)))
    n1.wait_send()


def output_kernel(nm_ref, wv_ref, q_ref, rh_ref, rl_ref, rtt_ref, norm_ref, onm_ref, onw_ref, onr_ref, nw, nr, sems):
    copies = [pltpu.make_async_copy(nm_ref, onm_ref, sems.at[0])]
    copies[0].start()
    nr[...] = rtt_ref[...] * norm_ref[0:1, :]
    copies.append(pltpu.make_async_copy(nr, onr_ref, sems.at[1]))
    copies[1].start()
    right = (rh_ref[...], rl_ref[...])
    for k in range(2):
        rows = pl.ds(256 * k, 256)
        nw[rows, :] = wv_ref[rows, :] - dot3(split(q_ref[rows, :]), right, 1, 0)
        copies.append(pltpu.make_async_copy(nw.at[rows], onw_ref.at[rows], sems.at[2 + k]))
        copies[2 + k].start()
    for cp in copies:
        cp.wait()


def hbm(array):
    return pltpu.with_memory_space_constraint(array, pltpu.HBM)


def body(momentum, gradient, weights, prior_right):
    vmem = pl.BlockSpec(memory_space=pltpu.VMEM)
    dma = pltpu.SemaphoreType.DMA
    inner = (
        pltpu.VMEM((BR, BC), F32),
        pltpu.VMEM((BR, BC), F32),
        pltpu.VMEM((BR, RANK), F32),
        pltpu.VMEM((RANK, BC), BF16),
        pltpu.VMEM((RANK, BC), BF16),
        pltpu.VMEM((BC, RANK), F32),
        pltpu.VMEM((8, RANK), F32),
    )
    factors = pl.pallas_call(
        factor_kernel,
        out_shape=inner,
        in_specs=[pl.BlockSpec(memory_space=pltpu.HBM)] * 4,
        out_specs=(vmem,) * len(inner),
        scratch_shapes=[
            pltpu.VMEM((2, 256, BC), F32),
            pltpu.VMEM((2, 256, BC), BF16),
            pltpu.VMEM((BC, RANK), F32),
            pltpu.VMEM((BR, BC), BF16),
            pltpu.VMEM((BR, BC), BF16),
            pltpu.VMEM((2, 256, HALF), F32),
            pltpu.VMEM((2, 256, HALF), F32),
            pltpu.VMEM((2, 256, HALF), F32),
            pltpu.VMEM((2, NX - 1, 64, HALF), F32),
            pltpu.VMEM((2, 64, HALF), F32),
            pltpu.VMEM((2, BR, HALF), F32),
            pltpu.VMEM((RANK, BR), F32),
            pltpu.VMEM((64, RANK), F32),
            pltpu.VMEM((NY - 1, 16, RANK), F32),
            pltpu.VMEM((NZ, 16, RANK), F32),
            pltpu.VMEM((NX, 64, RANK), F32),
            pltpu.VMEM((RANK, RANK), F32),
            pltpu.VMEM((RANK, BC), F32),
            pltpu.VMEM((RANK, BC), F32),
            pltpu.VMEM((NY - 1, 64, BC), F32),
            pltpu.VMEM((NZ - 1, 32, BC), F32),
            pltpu.VMEM((64, BC), F32),
            pltpu.VMEM((32, BC), F32),
            pltpu.VMEM((NY - 1, 8, BC), F32),
            pltpu.VMEM((NZ - 1, 8, BC), F32),
            pltpu.VMEM((8, BC), F32),
            pltpu.VMEM((2 * NX, 8, RANK), F32),
            dma((6,)),
            dma((2, 2)), dma((2, 2)),
            dma((2, 2)), dma((2, 2)),
            dma((3,)), dma((3,)),
            dma((len(CHUNKS), 4)), dma((len(CHUNKS), 4)),
            dma((1,)), dma((1,)),
        ],
        compiler_params=pltpu.CompilerParams(
            collective_id=0, has_side_effects=True, vmem_limit_bytes=40 * 1024 * 1024
        ),
        name="factors",
    )(hbm(momentum), hbm(gradient), hbm(weights), hbm(prior_right))
    return pl.pallas_call(
        output_kernel,
        out_shape=(
            jax.ShapeDtypeStruct((BR, BC), F32),
            jax.ShapeDtypeStruct((BR, BC), F32),
            jax.ShapeDtypeStruct((BC, RANK), F32),
        ),
        in_specs=[vmem] * len(inner),
        out_specs=(pl.BlockSpec(memory_space=pltpu.HBM),) * 3,
        scratch_shapes=[pltpu.VMEM((BR, BC), F32), pltpu.VMEM((BC, RANK), F32), dma((4,))],
        compiler_params=pltpu.CompilerParams(vmem_limit_bytes=40 * 1024 * 1024),
        name="outputs",
    )(*[pltpu.with_memory_space_constraint(a, pltpu.VMEM) for a in factors])


def solution(mesh):
    in_specs = (P("fsdp", "tensor"), P("fsdp", "tensor"), P("fsdp", "tensor"), P("tensor", None))
    out_specs = (P("fsdp", "tensor"), P("fsdp", "tensor"), P("tensor", None))
    return jax.shard_map(body, mesh=mesh, in_specs=in_specs, out_specs=out_specs, check_vma=False)
```
